32 devices in a mesh: ta: 4 (over z), ha: 4 (over x, core), wa: 2 (over y).
Axes of the slice: x: 2, y: 2, z: 4, core: 2. Of those that a mesh axis runs over, the one named last changes fastest.
Arguments:
- clip: bfloat16 [8, 16, 32, 256], P('ta', 'ha', 'wa'), may hold values from -6 to 6
- conv_weight: bfloat16 [6912, 256], replicated, may hold values from -0.078125 to 0.078125
- down_weight: bfloat16 [6912, 256], replicated, may hold values from -0.078125 to 0.078125
- out_cotangent: bfloat16 [4, 8, 16, 256], P('ta', 'ha', 'wa'), may hold values from -6 to 6
Outputs:
- grad_clip: bfloat16 [8, 16, 32, 256], P('ta', 'ha', 'wa')
- grad_conv: float32 [6912, 256], P(('ha', 'wa'), 'ta')
- grad_down: float32 [6912, 256], P(('ha', 'wa'), 'ta')
The draws below stay inside these ranges and needn't reach their ends.
All inputs are finite; a program needn't handle non-finite values.
Results may differ from the reference program's by a relative error of at most 0.014.
Values may be sent and summed in bfloat16 or wider, within the bound.
A program may use at most 64 MiB of HBM per device.

```python
import jax
import jax.numpy as jnp
from jax import lax

C = 256
NT = 8
NH = 16
NW = 32


def level_of(stream_key, shape, split, smallest, high):
    loudness = 1.0
    for position, blocks in split:
        draws = jax.random.uniform(jax.random.fold_in(jax.random.fold_in(stream_key, 6), position), (blocks,), jnp.float32, smallest / len(split), high / len(split))
        loudness = loudness * jnp.repeat(jnp.exp(draws), shape[position] // blocks).reshape((-1,) + (1,) * (len(shape) - 1 - position))
    return loudness


def bell_draw(own_key, dims, scale, most, pieces=(), dtype=jnp.bfloat16):
    drawn = scale * jax.random.normal(own_key, dims, jnp.float32)
    if pieces:
        drawn = drawn * level_of(own_key, dims, pieces, -0.22, 0.18)
    return jnp.clip(drawn, -most, most).astype(dtype)


def setup_inputs(seed: int = 0) -> dict:
    splits = jax.random.split(jax.random.key(seed), 5)
    return {
        "clip": bell_draw(splits[0], (NT, NH, NW, C), 1.0, 6.0, ((0, 4), (1, 4), (2, 2))),
        "conv_weight": bell_draw(splits[1], (27 * C, C), (27 * C) ** -0.5, 0.078125),
        "down_weight": bell_draw(splits[2], (27 * C, C), (27 * C) ** -0.5, 0.078125),
        "out_cotangent": bell_draw(splits[3], (NT // 2, NH // 2, NW // 2, C), 1.0, 6.0, ((0, 4), (1, 4), (2, 2))),
    }


def convolve(inputs, kernel, strides, padding):
    return lax.conv_general_dilated(inputs, kernel, strides, padding, dimension_numbers=('NDHWC', 'DHWIO', 'NDHWC'), precision=lax.Precision.HIGHEST)

def first_layer(inputs, kernel):
    return convolve(inputs, kernel, (1, 1, 1), [(2, 0), (1, 1), (1, 1)])

def down_layer(inputs, kernel):
    return convolve(inputs, kernel, (2, 2, 2), [(2, 0), (1, 0), (1, 0)])

def reference(clip, conv_weight, down_weight, out_cotangent):
    channels = clip.shape[-1]
    first_kernel = conv_weight.astype(jnp.float32).reshape(3, 3, 3, channels, channels)
    down_kernel = down_weight.astype(jnp.float32).reshape(3, 3, 3, channels, channels)
    clip_wide = clip.astype(jnp.float32)[None]
    pre_act = first_layer(clip_wide, first_kernel)
    activation = jax.nn.silu(pre_act).astype(jnp.bfloat16)
    outputs, down_pullback = jax.vjp(down_layer, activation.astype(jnp.float32), down_kernel)
    grad_act, grad_down = down_pullback(out_cotangent.astype(jnp.float32)[None])
    sigma = jax.nn.sigmoid(pre_act)
    grad_pre = (grad_act * sigma * (1.0 + pre_act * (1.0 - sigma))).astype(jnp.bfloat16)
    forward, first_pullback = jax.vjp(first_layer, clip_wide, first_kernel)
    grad_clip, grad_conv = first_pullback(grad_pre.astype(jnp.float32))
    return (grad_clip[0].astype(jnp.bfloat16), grad_conv.reshape(27 * channels, channels), grad_down.reshape(27 * channels, channels))
```

```python
import functools

import jax
import jax.numpy as jnp
from jax import lax
from jax.experimental import pallas as pl
from jax.experimental.pallas import tpu as pltpu
from jax.sharding import PartitionSpec as P

MESH = pl.DeviceIdType.MESH
SIDES = [(dh, dw) for dh in (-1, 0, 1) for dw in (-1, 0, 1) if (dh, dw) != (0, 0)]


def gather_kernel(sizes, x_ref, mid, rows, cols, diag, zs, zr, ps, pr):
    n_t, n_h, n_w = sizes
    t, h, w = lax.axis_index("ta"), lax.axis_index("ha"), lax.axis_index("wa")

    def exists(dh, dw):
        return (h + dh >= 0) & (h + dh < n_h) & (w + dw >= 0) & (w + dw < n_w)

    def slot(s, dh, dw):
        if dw == 0:
            return rows.at[s, 0 if dh > 0 else 1]
        if dh == 0:
            return cols.at[s, 0 if dw > 0 else 1]
        return diag.at[s, 0 if dh > 0 else 1, 0 if dw > 0 else 1]

    def part(dh, dw):
        if dw == 0:
            return pl.ds(0, 6) if dh < 0 else pl.ds(5, 6)
        if dh == 0:
            return pl.ds(4, 3)
        return pl.ds(4, 2) if dh < 0 else pl.ds(5, 2)

    barrier = pltpu.get_barrier_semaphore()
    count = n_t - 1
    for d in range(1, n_t):
        pl.semaphore_signal(
            barrier, inc=1, device_id=(lax.rem(t + d, n_t), h, w), device_id_type=MESH
        )
    for dh, dw in SIDES:
        there = exists(dh, dw)
        count = count + jnp.where(there, 1, 0)

        @pl.when(there)
        def _():
            pl.semaphore_signal(
                barrier, inc=1, device_id=(t, h + dh, w + dw), device_id_type=MESH
            )

    pl.semaphore_wait(barrier, count)

    along = []
    for d in range(1, n_t):
        copy = pltpu.make_async_remote_copy(
            src_ref=x_ref,
            dst_ref=mid.at[t],
            send_sem=zs.at[d - 1],
            recv_sem=zr.at[d - 1],
            device_id=(lax.rem(t + d, n_t), h, w),
            device_id_type=MESH,
        )
        copy.start()
        along.append(copy)

    def beside(d, s, i):
        dh, dw = SIDES[i]
        source = x_ref if d == 0 else mid.at[s]
        return pltpu.make_async_remote_copy(
            src_ref=source.at[part(dh, dw)],
            dst_ref=slot(s, dh, dw),
            send_sem=ps.at[d, i],
            recv_sem=pr.at[d, i],
            device_id=(t, h + dh, w + dw),
            device_id_type=MESH,
        )

    for d in range(n_t):
        s = lax.rem(t - d + n_t, n_t)
        if d > 0:
            along[d - 1].wait_recv()
        for i, (dh, dw) in enumerate(SIDES):

            @pl.when(exists(dh, dw))
            def _():
                beside(d, s, i).start()

        if d == 0:
            mid[t] = x_ref[...]
            for i, (dh, dw) in enumerate(SIDES):

                @pl.when(jnp.logical_not(exists(-dh, -dw)))
                def _():
                    for block in range(n_t):
                        target = slot(block, dh, dw)
                        target[...] = jnp.zeros(target.shape, target.dtype)

    for d in range(n_t):
        s = lax.rem(t - d + n_t, n_t)
        if d > 0:
            along[d - 1].wait_send()
        for i, (dh, dw) in enumerate(SIDES):

            @pl.when(exists(dh, dw))
            def _():
                beside(d, s, i).wait_send()

            @pl.when(exists(-dh, -dw))
            def _():
                beside(d, s, i).wait_recv()


def gather(x, sizes):
    n_t = sizes[0]
    tile = x.shape[1:]
    vmem = pl.BlockSpec(memory_space=pltpu.VMEM)
    shapes = [(n_t, 11), (n_t, 2, 6), (n_t, 2, 3), (n_t, 2, 2, 2)]
    return pl.pallas_call(
        functools.partial(gather_kernel, sizes),
        out_shape=[jax.ShapeDtypeStruct(shape + tile, x.dtype) for shape in shapes],
        in_specs=[vmem],
        out_specs=[vmem] * 4,
        scratch_shapes=[
            pltpu.SemaphoreType.DMA((n_t - 1,)),
            pltpu.SemaphoreType.DMA((n_t - 1,)),
            pltpu.SemaphoreType.DMA((n_t, 8)),
            pltpu.SemaphoreType.DMA((n_t, 8)),
        ],
        compiler_params=pltpu.CompilerParams(
            collective_id=0, has_side_effects=True, vmem_limit_bytes=32 * 2**20
        ),
    )(x)


def reduce_kernel(sizes, x_ref, out, pair, own, got, pair_sems, ss, rs):
    n_x, n_w = sizes
    t, h, w = lax.axis_index("ta"), lax.axis_index("ha"), lax.axis_index("wa")
    x, core = h // 2, lax.rem(h, 2)
    chips = n_x * n_w
    me = x * n_w + w

    def place(d):
        chip = lax.rem(me + d, chips)
        return (t, (chip // n_w) * 2 + core, lax.rem(chip, n_w))

    barrier = pltpu.get_barrier_semaphore()
    other = (t, h + 1 - 2 * core, w)
    pl.semaphore_signal(barrier, inc=1, device_id=other, device_id_type=MESH)
    for d in range(1, chips):
        pl.semaphore_signal(barrier, inc=1, device_id=place(d), device_id_type=MESH)
    pl.semaphore_wait(barrier, chips)

    def swap(d):
        chip = lax.rem(me + d, chips)
        return pltpu.make_async_remote_copy(
            src_ref=x_ref.at[chip // n_w, 1 - core, lax.rem(chip, n_w)],
            dst_ref=pair.at[chip],
            send_sem=pair_sems.at[0, d],
            recv_sem=pair_sems.at[1, d],
            device_id=other,
            device_id_type=MESH,
        )

    def send(d):
        return pltpu.make_async_remote_copy(
            src_ref=own.at[d],
            dst_ref=got.at[d],
            send_sem=ss.at[d],
            recv_sem=rs.at[d],
            device_id=place(d),
            device_id_type=MESH,
        )

    order = list(range(1, chips)) + [0]
    for d in order:
        swap(d).start()
    for d in order:
        chip = lax.rem(me + d, chips)
        swap(d).wait_recv()
        mine = x_ref[chip // n_w, core, lax.rem(chip, n_w)].astype(jnp.float32)
        both = mine + pair[chip].astype(jnp.float32)
        if d > 0:
            own[d] = both.astype(own.dtype)
            send(d).start()
        else:
            out[...] = both
    for d in range(1, chips):
        send(d).wait_recv()
        out[...] += got[d].astype(jnp.float32)
    for d in range(chips):
        swap(d).wait_send()
        if d > 0:
            send(d).wait_send()


def reduce_scatter(x, sizes):
    n_x, n_w = sizes
    chips = n_x * n_w
    share = x.shape[3:]
    vmem = pl.BlockSpec(memory_space=pltpu.VMEM)
    return pl.pallas_call(
        functools.partial(reduce_kernel, sizes),
        out_shape=jax.ShapeDtypeStruct(share, jnp.float32),
        in_specs=[vmem],
        out_specs=vmem,
        scratch_shapes=[
            pltpu.VMEM((chips,) + share, x.dtype),
            pltpu.VMEM((chips,) + share, x.dtype),
            pltpu.VMEM((chips,) + share, x.dtype),
            pltpu.SemaphoreType.DMA((2, chips)),
            pltpu.SemaphoreType.DMA((chips,)),
            pltpu.SemaphoreType.DMA((chips,)),
        ],
        compiler_params=pltpu.CompilerParams(
            collective_id=1, has_side_effects=True, vmem_limit_bytes=32 * 2**20
        ),
    )(x)


def convolve(inputs, kernel, specs, padding, lhs_step, rhs_step):
    return lax.conv_general_dilated(
        inputs,
        kernel,
        (1, 1, 1),
        padding,
        lhs_dilation=lhs_step,
        rhs_dilation=rhs_step,
        dimension_numbers=specs,
        preferred_element_type=jnp.float32,
    )


def local(clip, conv_weight, down_weight, out_cotangent):
    channels = clip.shape[-1]
    n_t, n_h, n_w = (lax.axis_size(axis) for axis in ("ta", "ha", "wa"))
    t, h, w = lax.axis_index("ta"), lax.axis_index("ha"), lax.axis_index("wa")
    share = channels // n_t
    first_kernel = conv_weight.reshape(3, 3, 3, channels, channels)
    down_kernel = down_weight.reshape(3, 3, 3, channels, channels)
    unit = (1, 1, 1)
    valid = [(0, 0), (0, 0), (0, 0)]
    forward_specs = ("NDHWC", "DHWIO", "NDHWC")
    back_specs = ("NDHWC", "DHWOI", "NDHWC")
    weight_specs = ("CDHWN", "IDHWO", "DHWNC")

    edges = jnp.concatenate([clip[:, :, :2], clip[:, :, -2:]], axis=2)
    packed = jnp.concatenate(
        [
            clip[:, :2].reshape(4, 16, channels),
            edges[:, :2].reshape(1, 16, channels),
            out_cotangent.reshape(1, 16, channels),
            edges[:, 2:].reshape(1, 16, channels),
            clip[:, 2:].reshape(4, 16, channels),
        ],
        axis=0,
    )
    mid, rows, cols, diag = gather(packed, (n_t, n_h, n_w))
    frames = 2 * n_t

    def half(chunk):
        return chunk.reshape(frames, 2, 16, channels)

    def edge(chunk):
        return chunk.reshape(frames, 2, 4, channels)

    def coarse(chunk):
        return chunk.reshape(n_t, 2, 8, channels)

    centre = jnp.concatenate(
        [half(rows[:, 0, 2:6]), half(mid[:, 0:4]), half(mid[:, 7:11]), half(rows[:, 1, 0:4])],
        axis=1,
    )
    left, right = (
        jnp.concatenate(
            [
                edge(diag[:, 0, side, 1]),
                edge(cols[:, side, 0]),
                edge(cols[:, side, 2]),
                edge(diag[:, 1, side, 0]),
            ],
            axis=1,
        )
        for side in (0, 1)
    )
    clip_ext = jnp.concatenate([left[:, :, 2:], centre, right[:, :, :2]], axis=2)
    cot_rows = [
        jnp.concatenate([coarse(a), coarse(b), coarse(c)], axis=2)
        for a, b, c in (
            (diag[:, 0, 0, 0], rows[:, 0, 0], diag[:, 0, 1, 0]),
            (cols[:, 0, 1], mid[:, 5], cols[:, 1, 1]),
            (diag[:, 1, 0, 1], rows[:, 1, 5], diag[:, 1, 1, 1]),
        )
    ]
    cot_ext = jnp.concatenate(cot_rows, axis=1)[:, 1:5, 7:17]
    cot_mid = coarse(mid[:, 5])

    row = lax.broadcasted_iota(jnp.int32, (1, 6, 18, 1), 1) + (h * 4 - 1)
    col = lax.broadcasted_iota(jnp.int32, (1, 6, 18, 1), 2) + (w * 16 - 1)
    inside = (row >= 0) & (row < 4 * n_h) & (col >= 0) & (col < 16 * n_w)
    pre_act = convolve(
        clip_ext[None], first_kernel, forward_specs, [(2, 0), (0, 0), (0, 0)], unit, unit
    )[0]
    grad_act = convolve(
        cot_ext[None],
        down_kernel[::-1, ::-1, ::-1],
        back_specs,
        [(0, 3), (0, 1), (0, 1)],
        (2, 2, 2),
        unit,
    )[0]
    sigma = jax.nn.sigmoid(pre_act)
    activation = jnp.where(inside, pre_act * sigma, 0.0).astype(jnp.bfloat16)
    grad_pre = jnp.where(
        inside, grad_act * sigma * (1.0 + pre_act * (1.0 - sigma)), 0.0
    ).astype(jnp.bfloat16)

    start = t * share

    def blocks(values, depth):
        ahead = jnp.pad(values, ((2, 0), (0, 0), (0, 0), (0, 0)))
        return jnp.stack([ahead[2 * i : 2 * i + depth] for i in range(n_t)])

    act_blocks = blocks(activation[:, :5, :17], 3)
    clip_blocks = blocks(clip_ext[:, 1:7, 1:19], 4)
    cot_blocks = lax.dynamic_slice_in_dim(cot_mid, start, share, 3)[:, None]
    grad_mid = lax.dynamic_slice_in_dim(grad_pre[:, 1:5, 1:17], start, share, 3)
    grad_blocks = grad_mid.reshape(n_t, 2, 4, 16, share)
    grad_down = convolve(act_blocks, cot_blocks, weight_specs, valid, unit, (2, 2, 2))
    grad_conv = convolve(clip_blocks, grad_blocks, weight_specs, valid, unit, unit)
    terms = jnp.concatenate(
        [grad_conv.reshape(27 * channels, share), grad_down.reshape(27 * channels, share)], axis=1
    ).astype(jnp.bfloat16)
    terms = terms.reshape(n_h // 2, 2, n_w, 27 * channels // (n_h * n_w), 2 * share)
    total = reduce_scatter(terms, (n_h // 2, n_w))

    later = jnp.pad(grad_pre, ((0, 2), (0, 0), (0, 0), (0, 0)))
    grad_ext = lax.dynamic_slice_in_dim(later, 2 * t, 4, 0)
    grad_clip = convolve(
        grad_ext[None], first_kernel[::-1, ::-1, ::-1], back_specs, valid, unit, unit
    )[0].astype(jnp.bfloat16)
    return (grad_clip, total[:, :share], total[:, share:])


def solution(mesh):
    return jax.shard_map(
        local,
        mesh=mesh,
        in_specs=(P("ta", "ha", "wa", None), P(), P(), P("ta", "ha", "wa", None)),
        out_specs=(P("ta", "ha", "wa", None), P(("ha", "wa"), "ta"), P(("ha", "wa"), "ta")),
        check_vma=False,
    )
```

```python
import functools

import jax
import jax.numpy as jnp
from jax import lax
from jax.experimental import pallas as pl
from jax.experimental.pallas import tpu as pltpu
from jax.sharding import PartitionSpec as P

MESH = pl.DeviceIdType.MESH
SIDES = [(dh, dw) for dh in (-1, 0, 1) for dw in (-1, 0, 1) if (dh, dw) != (0, 0)]


def gather_kernel(sizes, x_ref, mid, rows, cols, diag, zs, zr, ps, pr):
    n_t, n_h, n_w = sizes
    t, h, w = lax.axis_index("ta"), lax.axis_index("ha"), lax.axis_index("wa")

    def exists(dh, dw):
        return (h + dh >= 0) & (h + dh < n_h) & (w + dw >= 0) & (w + dw < n_w)

    def slot(s, dh, dw):
        if dw == 0:
            return rows.at[s, 0 if dh > 0 else 1]
        if dh == 0:
            return cols.at[s, 0 if dw > 0 else 1]
        return diag.at[s, 0 if dh > 0 else 1, 0 if dw > 0 else 1]

    def part(dh, dw):
        if dw == 0:
            return pl.ds(0, 6) if dh < 0 else pl.ds(5, 6)
        if dh == 0:
            return pl.ds(4, 3)
        return pl.ds(4, 2) if dh < 0 else pl.ds(5, 2)

    barrier = pltpu.get_barrier_semaphore()
    count = n_t - 1
    for d in range(1, n_t):
        pl.semaphore_signal(
            barrier, inc=1, device_id=(lax.rem(t + d, n_t), h, w), device_id_type=MESH
        )
    for dh, dw in SIDES:
        there = exists(dh, dw)
        count = count + jnp.where(there, 1, 0)

        @pl.when(there)
        def _():
            pl.semaphore_signal(
                barrier, inc=1, device_id=(t, h + dh, w + dw), device_id_type=MESH
            )

    pl.semaphore_wait(barrier, count)

    along = []
    for d in range(1, n_t):
        copy = pltpu.make_async_remote_copy(
            src_ref=x_ref,
            dst_ref=mid.at[t],
            send_sem=zs.at[d - 1],
            recv_sem=zr.at[d - 1],
            device_id=(lax.rem(t + d, n_t), h, w),
            device_id_type=MESH,
        )
        copy.start()
        along.append(copy)

    def beside(d, s, i):
        dh, dw = SIDES[i]
        source = x_ref if d == 0 else mid.at[s]
        return pltpu.make_async_remote_copy(
            src_ref=source.at[part(dh, dw)],
            dst_ref=slot(s, dh, dw),
            send_sem=ps.at[d, i],
            recv_sem=pr.at[d, i],
            device_id=(t, h + dh, w + dw),
            device_id_type=MESH,
        )

    for d in range(n_t):
        s = lax.rem(t - d + n_t, n_t)
        if d > 0:
            along[d - 1].wait_recv()
        for i, (dh, dw) in enumerate(SIDES):

            @pl.when(exists(dh, dw))
            def _():
                beside(d, s, i).start()

        if d == 0:
            mid[t] = x_ref[...]
            for i, (dh, dw) in enumerate(SIDES):

                @pl.when(jnp.logical_not(exists(-dh, -dw)))
                def _():
                    for block in range(n_t):
                        target = slot(block, dh, dw)
                        target[...] = jnp.zeros(target.shape, target.dtype)

    for d in range(n_t):
        s = lax.rem(t - d + n_t, n_t)
        if d > 0:
            along[d - 1].wait_send()
        for i, (dh, dw) in enumerate(SIDES):

            @pl.when(exists(dh, dw))
            def _():
                beside(d, s, i).wait_send()

            @pl.when(exists(-dh, -dw))
            def _():
                beside(d, s, i).wait_recv()


def gather(x, sizes):
    n_t = sizes[0]
    tile = x.shape[1:]
    vmem = pl.BlockSpec(memory_space=pltpu.VMEM)
    shapes = [(n_t, 11), (n_t, 2, 6), (n_t, 2, 3), (n_t, 2, 2, 2)]
    return pl.pallas_call(
        functools.partial(gather_kernel, sizes),
        out_shape=[jax.ShapeDtypeStruct(shape + tile, x.dtype) for shape in shapes],
        in_specs=[vmem],
        out_specs=[vmem] * 4,
        scratch_shapes=[
            pltpu.SemaphoreType.DMA((n_t - 1,)),
            pltpu.SemaphoreType.DMA((n_t - 1,)),
            pltpu.SemaphoreType.DMA((n_t, 8)),
            pltpu.SemaphoreType.DMA((n_t, 8)),
        ],
        compiler_params=pltpu.CompilerParams(
            collective_id=0, has_side_effects=True, vmem_limit_bytes=32 * 2**20
        ),
    )(x)


def reduce_kernel(sizes, x_ref, out, pair, own, got, pair_sems, ss, rs):
    n_x, n_w = sizes
    t, h, w = lax.axis_index("ta"), lax.axis_index("ha"), lax.axis_index("wa")
    x, core = h // 2, lax.rem(h, 2)
    chips = n_x * n_w
    me = x * n_w + w

    def place(d):
        chip = lax.rem(me + d, chips)
        return (t, (chip // n_w) * 2 + core, lax.rem(chip, n_w))

    barrier = pltpu.get_barrier_semaphore()
    other = (t, h + 1 - 2 * core, w)
    pl.semaphore_signal(barrier, inc=1, device_id=other, device_id_type=MESH)
    for d in range(1, chips):
        pl.semaphore_signal(barrier, inc=1, device_id=place(d), device_id_type=MESH)
    pl.semaphore_wait(barrier, chips)

    def swap(d):
        chip = lax.rem(me + d, chips)
        return pltpu.make_async_remote_copy(
            src_ref=x_ref.at[chip // n_w, 1 - core, lax.rem(chip, n_w)],
            dst_ref=pair.at[chip],
            send_sem=pair_sems.at[0, d],
            recv_sem=pair_sems.at[1, d],
            device_id=other,
            device_id_type=MESH,
        )

    def send(d):
        return pltpu.make_async_remote_copy(
            src_ref=own.at[d],
            dst_ref=got.at[d],
            send_sem=ss.at[d],
            recv_sem=rs.at[d],
            device_id=place(d),
            device_id_type=MESH,
        )

    order = list(range(1, chips)) + [0]
    for d in order:
        swap(d).start()
    for d in order:
        chip = lax.rem(me + d, chips)
        swap(d).wait_recv()
        mine = x_ref[chip // n_w, core, lax.rem(chip, n_w)].astype(jnp.float32)
        both = mine + pair[chip].astype(jnp.float32)
        if d > 0:
            own[d] = both.astype(own.dtype)
            send(d).start()
        else:
            out[...] = both
    for d in range(1, chips):
        send(d).wait_recv()
        out[...] += got[d].astype(jnp.float32)
    for d in range(chips):
        swap(d).wait_send()
        if d > 0:
            send(d).wait_send()


def reduce_scatter(x, sizes):
    n_x, n_w = sizes
    chips = n_x * n_w
    share = x.shape[3:]
    vmem = pl.BlockSpec(memory_space=pltpu.VMEM)
    return pl.pallas_call(
        functools.partial(reduce_kernel, sizes),
        out_shape=jax.ShapeDtypeStruct(share, jnp.float32),
        in_specs=[vmem],
        out_specs=vmem,
        scratch_shapes=[
            pltpu.VMEM((chips,) + share, x.dtype),
            pltpu.VMEM((chips,) + share, x.dtype),
            pltpu.VMEM((chips,) + share, x.dtype),
            pltpu.SemaphoreType.DMA((2, chips)),
            pltpu.SemaphoreType.DMA((chips,)),
            pltpu.SemaphoreType.DMA((chips,)),
        ],
        compiler_params=pltpu.CompilerParams(
            collective_id=1, has_side_effects=True, vmem_limit_bytes=32 * 2**20
        ),
    )(x)


NT = (((1,), (1,)), ((), ()))


def dot(lhs, rhs):
    return jnp.dot(lhs, rhs, preferred_element_type=jnp.float32)


def dot_nt(lhs, rhs):
    return lax.dot_general(lhs, rhs, NT, preferred_element_type=jnp.float32)


def compute_kernel(
    sizes, mid, rows, cols, diag, k1, kd, terms, grad_clip,
    wide, even, odd, parts, fine, act, grad, moved, dilated, own,
):
    n_t, n_h, n_w = sizes
    frames = 2 * n_t
    t, h, w = lax.axis_index("ta"), lax.axis_index("ha"), lax.axis_index("wa")
    f32, b16 = jnp.float32, jnp.bfloat16
    ch = mid.shape[-1]
    share = ch // n_t

    wide[0:2] = jnp.zeros((2, 8, 24, ch), f32)
    grad[frames : frames + 2] = jnp.zeros((2, 6, 24, ch), f32)
    act[0:1] = jnp.zeros((1,) + act.shape[1:], f32)
    dilated[n_t : n_t + 1] = jnp.zeros((1,) + dilated.shape[1:], f32)
    moved[...] = jnp.zeros(moved.shape, f32)

    out_at = lax.broadcasted_iota(jnp.int32, (72, 24), 0)
    in_at = lax.broadcasted_iota(jnp.int32, (72, 24), 1)
    tap = jnp.where(out_at >= 48, 2, jnp.where(out_at >= 24, 1, 0))
    reach = out_at - 24 * tap - tap
    hit = (reach == 2 * (in_at - 8))
    select = jnp.where(hit, 1.0, 0.0).astype(b16)
    select_own = jnp.where(hit & (in_at >= 8) & (in_at < 16), 1.0, 0.0).astype(b16)

    @pl.loop(0, n_t)
    def _(s):
        for f in range(2):
            for r in range(2):
                at, k = 2 + 2 * s + f, 2 * f + r
                wide[at, r, 2:18] = rows[s, 0, 2 + k].astype(f32)
                wide[at, 2 + r, 2:18] = mid[s, k].astype(f32)
                wide[at, 4 + r, 2:18] = mid[s, 7 + k].astype(f32)
                wide[at, 6 + r, 2:18] = rows[s, 1, k].astype(f32)
        for side in range(2):
            strips = (diag[s, 0, side, 1], cols[s, side, 0], cols[s, side, 2], diag[s, 1, side, 0])
            for n, strip in enumerate(strips):
                strip = strip.astype(f32)
                for f in range(2):
                    for r in range(2):
                        first = 4 * (2 * f + r) + 2 - 2 * side
                        wide[2 + 2 * s + f, 2 * n + r, 18 * side : 18 * side + 2] = strip[
                            first : first + 2
                        ]
        middle = (
            (diag[s, 0, 0, 0], rows[s, 0, 0], diag[s, 0, 1, 0]),
            (cols[s, 0, 1], mid[s, 5], cols[s, 1, 1]),
            (diag[s, 1, 0, 1], rows[s, 1, 5], diag[s, 1, 1, 1]),
        )
        for n, (block, r) in enumerate(((0, 1), (1, 0), (1, 1), (2, 0))):
            line = jnp.concatenate(
                [x.astype(f32)[8 * r : 8 * r + 8] for x in middle[block]], axis=0
            ).astype(b16)
            spread = dot(select, line)
            for c in range(3):
                dilated[s, n, c] = spread[24 * c : 24 * c + 24]
            if block == 1:
                spread = dot(select_own, line)
                for c in range(3):
                    own[c, s, r] = spread[24 * c : 24 * c + 24]

    @pl.loop(0, frames + 2)
    def _(f):
        even[f] = wide[f].reshape(192, ch).astype(b16)
        odd[f] = wide[f, 1:7].reshape(144, ch).astype(b16)

    def shifted(f, count, b):
        if b == 1:
            return odd[pl.ds(f, count)].reshape(count * 144, ch)
        return even[pl.ds(f, count), 24 * b : 24 * b + 144].reshape(count * 144, ch)

    def weight(ref, a, b, c):
        return ref[pl.ds(((a * 3 + b) * 3 + c) * ch, ch), :]

    @pl.loop(0, n_t)
    def _(s):
        for c in range(3):
            total = jnp.zeros((288, ch), f32)
            for a in range(3):
                for b in range(3):
                    total += dot(shifted(2 * s + a, 2, b), weight(k1, a, b, c))
            parts[c, pl.ds(2 * s, 2), :, 0:24] = total.reshape(2, 6, 24, ch)

    for pt in range(2):
        for ph in range(2):
            total = jnp.zeros((n_t * 72, ch), f32)
            for a in (1,) if pt else (0, 2):
                for b in (1,) if ph else (0, 2):
                    j = 0 if a == 2 else 1
                    r = 0 if b == 2 else 1
                    for c in range(3):
                        lhs = dilated[j : j + n_t, r : r + 3, c].reshape(n_t * 72, ch)
                        total += dot_nt(lhs.astype(b16), weight(kd, a, b, c))
            fine[:, pt, :, ph] = total.reshape(n_t, 3, 24, ch)

    row = lax.broadcasted_iota(jnp.int32, (6, 24, ch), 0) + (h * 4 - 1)
    place = lax.broadcasted_iota(jnp.int32, (6, 24, ch), 1)
    col = place + (w * 16 - 1)
    inside = (row >= 0) & (row < 4 * n_h) & (col >= 0) & (col < 16 * n_w) & (place < 18)

    @pl.loop(0, n_t)
    def _(s):
        for k in range(2):
            f = 2 * s + k
            pre = parts[0, f, :, 0:24] + parts[1, f, :, 1:25] + parts[2, f, :, 2:26]
            sigma = 1.0 / (1.0 + jnp.exp(-pre))
            value = jnp.where(inside, pre * sigma, 0.0)
            act[s + 1, k] = value.astype(b16).astype(f32).reshape(3, 2, 24, ch)
            back = fine[s, k].reshape(6, 24, ch) * sigma * (1.0 + pre * (1.0 - sigma))
            grad[f] = jnp.where(inside, back, 0.0).astype(b16).astype(f32)
            centre = grad[f, 1:5, 1:17]
            for c in range(3):
                moved[c, f, :, 1 + c : 17 + c] = centre

    pick = (
        lax.broadcasted_iota(jnp.int32, (share, ch), 1)
        == lax.broadcasted_iota(jnp.int32, (share, ch), 0) + t * share
    )
    pick = jnp.where(pick, 1.0, 0.0).astype(b16)
    conv_side = jnp.concatenate(
        [dot_nt(pick, moved[c].reshape(frames * 96, ch).astype(b16)) for c in range(3)], axis=0
    ).astype(b16)
    down_side = jnp.concatenate(
        [dot_nt(pick, own[c].reshape(n_t * 48, ch).astype(b16)) for c in range(3)], axis=0
    ).astype(b16)
    for a in range(3):
        for b in range(3):
            if b == 1:
                lhs = even[a : a + frames, 48:144]
            else:
                lhs = odd[a : a + frames, 24 * b : 24 * b + 96]
            conv = dot(conv_side, lhs.reshape(frames * 96, ch))
            lhs = act[a // 2 : a // 2 + n_t, a % 2, b // 2 : b // 2 + 2, b % 2]
            down = dot(down_side, lhs.reshape(n_t * 48, ch).astype(b16))
            for c in range(3):
                cut = slice(share * c, share * (c + 1))
                both = jnp.concatenate([conv[cut], down[cut]], axis=0)
                at = ((a * 3 + b) * 3 + c) * ch
                terms[at : at + ch] = both.T.astype(b16)

    sums = [jnp.zeros((192, ch), f32) for _ in range(3)]
    for c in range(3):
        for a in range(3):
            for b in range(3):
                lhs = grad[pl.ds(2 * t + 2 - a, 2), 2 - b : 6 - b].reshape(192, ch)
                sums[c] += dot_nt(lhs.astype(b16), weight(k1, a, b, c))
        parts[c, 0:2, 0:4, 0:24] = sums[c].reshape(2, 4, 24, ch)
    result = (
        parts[0, 0:2, 0:4, 2:18] + parts[1, 0:2, 0:4, 1:17] + parts[2, 0:2, 0:4, 0:16]
    )
    grad_clip[...] = result.astype(b16)


def compute(mid, rows, cols, diag, conv_weight, down_weight, sizes):
    n_t = sizes[0]
    frames = 2 * n_t
    ch = mid.shape[-1]
    f32, b16 = jnp.float32, jnp.bfloat16
    vmem = pl.BlockSpec(memory_space=pltpu.VMEM)
    return pl.pallas_call(
        functools.partial(compute_kernel, sizes),
        out_shape=[
            jax.ShapeDtypeStruct((27 * ch, 2 * ch // n_t), b16),
            jax.ShapeDtypeStruct((2, 4, 16, ch), b16),
        ],
        in_specs=[vmem] * 6,
        out_specs=[vmem] * 2,
        scratch_shapes=[
            pltpu.VMEM((frames + 2, 8, 24, ch), f32),
            pltpu.VMEM((frames + 2, 192, ch), b16),
            pltpu.VMEM((frames + 2, 144, ch), b16),
            pltpu.VMEM((3, frames, 6, 32, ch), f32),
            pltpu.VMEM((n_t, 2, 3, 2, 24, ch), f32),
            pltpu.VMEM((n_t + 1, 2, 3, 2, 24, ch), f32),
            pltpu.VMEM((frames + 2, 6, 24, ch), f32),
            pltpu.VMEM((3, frames, 4, 24, ch), f32),
            pltpu.VMEM((n_t + 1, 4, 3, 24, ch), f32),
            pltpu.VMEM((3, n_t, 2, 24, ch), f32),
        ],
        compiler_params=pltpu.CompilerParams(vmem_limit_bytes=56 * 2**20),
    )(mid, rows, cols, diag, conv_weight, down_weight)


def local(clip, conv_weight, down_weight, out_cotangent):
    channels = clip.shape[-1]
    n_t, n_h, n_w = (lax.axis_size(axis) for axis in ("ta", "ha", "wa"))
    share = channels // n_t
    edges = jnp.concatenate([clip[:, :, :2], clip[:, :, -2:]], axis=2)
    packed = jnp.concatenate(
        [
            clip[:, :2].reshape(4, 16, channels),
            edges[:, :2].reshape(1, 16, channels),
            out_cotangent.reshape(1, 16, channels),
            edges[:, 2:].reshape(1, 16, channels),
            clip[:, 2:].reshape(4, 16, channels),
        ],
        axis=0,
    )
    mid, rows, cols, diag = gather(packed, (n_t, n_h, n_w))
    terms, grad_clip = compute(
        mid, rows, cols, diag, conv_weight, down_weight, (n_t, n_h, n_w)
    )
    terms = terms.reshape(n_h // 2, 2, n_w, 27 * channels // (n_h * n_w), 2 * share)
    total = reduce_scatter(terms, (n_h // 2, n_w))

    return (grad_clip, total[:, :share], total[:, share:])


def solution(mesh):
    return jax.shard_map(
        local,
        mesh=mesh,
        in_specs=(P("ta", "ha", "wa", None), P(), P(), P("ta", "ha", "wa", None)),
        out_specs=(P("ta", "ha", "wa", None), P(("ha", "wa"), "ta"), P(("ha", "wa"), "ta")),
        check_vma=False,
    )
```

```python
import functools

import jax
import jax.numpy as jnp
from jax import lax
from jax.experimental import pallas as pl
from jax.experimental.pallas import tpu as pltpu
from jax.sharding import PartitionSpec as P

MESH = pl.DeviceIdType.MESH
SIDES = [(dh, dw) for dh in (-1, 0, 1) for dw in (-1, 0, 1) if (dh, dw) != (0, 0)]
NT = (((1,), (1,)), ((), ()))


def dot(lhs, rhs):
    return jnp.dot(lhs, rhs, preferred_element_type=jnp.float32)


def dot_nt(lhs, rhs):
    return lax.dot_general(lhs, rhs, NT, preferred_element_type=jnp.float32)


def kernel(
    sizes, clip, cot, k1_hbm, kd_hbm, grad_clip, grad_conv, grad_down,
    k1, kd, mid, edge, strip_f32, rows, cols, diag,
    wide, even, odd, parts, fine, act, grad, moved, dilated, own_cot,
    flat, terms, pair, both, got,
    load, zs, zr, ps, pr, pair_sems, ss, rs,
):
    n_t, n_h, n_w = sizes
    frames = 2 * n_t
    t, h, w = lax.axis_index("ta"), lax.axis_index("ha"), lax.axis_index("wa")
    f32, b16 = jnp.float32, jnp.bfloat16
    ch = clip.shape[-1]
    share = ch // n_t
    peers = n_h * n_w
    chips = peers // 2
    core = lax.rem(h, 2)
    me = (h // 2) * n_w + w

    loads = [
        pltpu.make_async_copy(k1_hbm, k1, load.at[0]),
        pltpu.make_async_copy(kd_hbm, kd, load.at[1]),
    ]
    for copy in loads:
        copy.start()

    barrier = pltpu.get_barrier_semaphore()
    for d in range(1, n_t):
        pl.semaphore_signal(
            barrier, inc=1, device_id=(lax.rem(t + d, n_t), h, w), device_id_type=MESH
        )
    for d in range(1, peers):
        peer = lax.rem(h * n_w + w + d, peers)
        pl.semaphore_signal(
            barrier, inc=1, device_id=(t, peer // n_w, lax.rem(peer, n_w)), device_id_type=MESH
        )

    def exists(dh, dw):
        return (h + dh >= 0) & (h + dh < n_h) & (w + dw >= 0) & (w + dw < n_w)

    def slot(s, dh, dw):
        if dw == 0:
            return rows.at[s, 0 if dh > 0 else 1]
        if dh == 0:
            return cols.at[s, 0 if dw > 0 else 1]
        return diag.at[s, 0 if dh > 0 else 1, 0 if dw > 0 else 1]

    def piece(s, dh, dw):
        if dw == 0:
            return mid.at[s, pl.ds(0, 5) if dh < 0 else pl.ds(4, 5)]
        if dh == 0:
            return edge.at[s]
        return edge.at[s, pl.ds(0, 2) if dh < 0 else pl.ds(1, 2)]

    for f in range(2):
        for r in range(2):
            mid[t, 2 * f + r] = clip[f, r]
            mid[t, 5 + 2 * f + r] = clip[f, 2 + r]
    mid[t, 4] = cot[0].reshape(16, ch)

    def pack(s):
        for p in range(2):
            for k in range(4):
                line = mid[s, 5 * p + k].astype(f32)
                strip_f32[p, 4 * k : 4 * k + 2] = line[0:2]
                strip_f32[p, 4 * k + 2 : 4 * k + 4] = line[14:16]
            edge[s, 2 * p] = strip_f32[p].astype(b16)
        edge[s, 1] = mid[s, 4]

    pack(t)
    pl.semaphore_wait(barrier, n_t + peers - 2)

    along = []
    for d in range(1, n_t):
        copy = pltpu.make_async_remote_copy(
            src_ref=mid.at[t],
            dst_ref=mid.at[t],
            send_sem=zs.at[d - 1],
            recv_sem=zr.at[d - 1],
            device_id=(lax.rem(t + d, n_t), h, w),
            device_id_type=MESH,
        )
        copy.start()
        along.append(copy)

    def landing(d):
        s = lax.rem(t - d + n_t, n_t)
        return pltpu.make_async_remote_copy(
            src_ref=mid.at[s],
            dst_ref=mid.at[s],
            send_sem=zs.at[d - 1],
            recv_sem=zr.at[d - 1],
            device_id=(lax.rem(t + d, n_t), h, w),
            device_id_type=MESH,
        )

    def beside(d, i):
        dh, dw = SIDES[i]
        s = lax.rem(t - d + n_t, n_t)
        return pltpu.make_async_remote_copy(
            src_ref=piece(s, dh, dw),
            dst_ref=slot(s, dh, dw),
            send_sem=ps.at[d, i],
            recv_sem=pr.at[d, i],
            device_id=(t, h + dh, w + dw),
            device_id_type=MESH,
        )

    def spread_out(d):
        for i, (dh, dw) in enumerate(SIDES):

            @pl.when(exists(dh, dw))
            def _():
                beside(d, i).start()

    def collect(d):
        for i, (dh, dw) in enumerate(SIDES):

            @pl.when(exists(-dh, -dw))
            def _():
                beside(d, i).wait_recv()

    spread_out(0)
    for i, (dh, dw) in enumerate(SIDES):

        @pl.when(jnp.logical_not(exists(-dh, -dw)))
        def _():
            for block in range(n_t):
                target = slot(block, dh, dw)
                target[...] = jnp.zeros(target.shape, target.dtype)

    wide[0:2] = jnp.zeros((2, 8, 24, ch), f32)
    grad[frames : frames + 2] = jnp.zeros((2, 6, 24, ch), f32)
    act[0:1] = jnp.zeros((1,) + act.shape[1:], f32)
    dilated[n_t : n_t + 1] = jnp.zeros((1,) + dilated.shape[1:], f32)
    moved[...] = jnp.zeros(moved.shape, f32)

    out_at = lax.broadcasted_iota(jnp.int32, (72, 24), 0)
    in_at = lax.broadcasted_iota(jnp.int32, (72, 24), 1)
    tap = jnp.where(out_at >= 48, 2, jnp.where(out_at >= 24, 1, 0))
    reach = out_at - 24 * tap - tap
    hit = (reach == 2 * (in_at - 8))
    select = jnp.where(hit, 1.0, 0.0).astype(b16)
    select_own = jnp.where(hit & (in_at >= 8) & (in_at < 16), 1.0, 0.0).astype(b16)

    def fill(s):
        for f in range(2):
            for r in range(2):
                at, k = 2 + 2 * s + f, 2 * f + r
                wide[at, r, 2:18] = rows[s, 0, 1 + k].astype(f32)
                wide[at, 2 + r, 2:18] = mid[s, k].astype(f32)
                wide[at, 4 + r, 2:18] = mid[s, 5 + k].astype(f32)
                wide[at, 6 + r, 2:18] = rows[s, 1, k].astype(f32)
        for side in range(2):
            strips = (diag[s, 0, side, 1], cols[s, side, 0], cols[s, side, 2], diag[s, 1, side, 0])
            for n, strip in enumerate(strips):
                strip = strip.astype(f32)
                for f in range(2):
                    for r in range(2):
                        first = 4 * (2 * f + r) + 2 - 2 * side
                        wide[2 + 2 * s + f, 2 * n + r, 18 * side : 18 * side + 2] = strip[
                            first : first + 2
                        ]
        middle = (
            (diag[s, 0, 0, 0], rows[s, 0, 0], diag[s, 0, 1, 0]),
            (cols[s, 0, 1], mid[s, 4], cols[s, 1, 1]),
            (diag[s, 1, 0, 1], rows[s, 1, 4], diag[s, 1, 1, 1]),
        )
        for n, (block, r) in enumerate(((0, 1), (1, 0), (1, 1), (2, 0))):
            line = jnp.concatenate(
                [x.astype(f32)[8 * r : 8 * r + 8] for x in middle[block]], axis=0
            ).astype(b16)
            spread = dot(select, line)
            for c in range(3):
                dilated[s, n, c] = spread[24 * c : 24 * c + 24]
            if block == 1:
                spread = dot(select_own, line)
                for c in range(3):
                    own_cot[c, s, r] = spread[24 * c : 24 * c + 24]

    for d in range(1, n_t + 1):
        if d < n_t:
            landing(d).wait_recv()
            pack(lax.rem(t - d + n_t, n_t))
            spread_out(d)
        collect(d - 1)
        fill(lax.rem(t - d + 1 + n_t, n_t))

    @pl.loop(0, frames + 2)
    def _(f):
        even[f] = wide[f].reshape(192, ch).astype(b16)
        odd[f] = wide[f, 1:7].reshape(144, ch).astype(b16)

    def shifted(f, count, b):
        if b == 1:
            return odd[pl.ds(f, count)].reshape(count * 144, ch)
        return even[pl.ds(f, count), 24 * b : 24 * b + 144].reshape(count * 144, ch)

    def weight(ref, a, b, c):
        return ref[pl.ds(((a * 3 + b) * 3 + c) * ch, ch), :]

    loads[0].wait()

    @pl.loop(0, n_t)
    def _(s):
        for c in range(3):
            total = jnp.zeros((288, ch), f32)
            for a in range(3):
                for b in range(3):
                    total += dot(shifted(2 * s + a, 2, b), weight(k1, a, b, c))
            parts[c, pl.ds(2 * s, 2), :, 0:24] = total.reshape(2, 6, 24, ch)

    row = lax.broadcasted_iota(jnp.int32, (6, 24, ch), 0) + (h * 4 - 1)
    place = lax.broadcasted_iota(jnp.int32, (6, 24, ch), 1)
    col = place + (w * 16 - 1)
    inside = (row >= 0) & (row < 4 * n_h) & (col >= 0) & (col < 16 * n_w) & (place < 18)

    @pl.loop(0, n_t)
    def _(s):
        for k in range(2):
            f = 2 * s + k
            pre = parts[0, f, :, 0:24] + parts[1, f, :, 1:25] + parts[2, f, :, 2:26]
            parts[0, f, :, 0:24] = pre
            sigma = 1.0 / (1.0 + jnp.exp(-pre))
            value = jnp.where(inside, pre * sigma, 0.0)
            act[s + 1, k] = value.astype(b16).astype(f32).reshape(3, 2, 24, ch)

    pick = (
        lax.broadcasted_iota(jnp.int32, (share, ch), 1)
        == lax.broadcasted_iota(jnp.int32, (share, ch), 0) + t * share
    )
    pick = jnp.where(pick, 1.0, 0.0).astype(b16)
    width = 27 * ch // peers
    down_side = jnp.concatenate(
        [dot_nt(pick, own_cot[c].reshape(n_t * 48, ch).astype(b16)) for c in range(3)], axis=0
    ).astype(b16)
    for a in range(3):
        for b in range(3):
            lhs = act[a // 2 : a // 2 + n_t, a % 2, b // 2 : b // 2 + 2, b % 2]
            down = dot(down_side, lhs.reshape(n_t * 48, ch).astype(b16))
            for c in range(3):
                at = ((a * 3 + b) * 3 + c) * ch
                flat[0, :, at : at + ch] = down[share * c : share * (c + 1)]

    def place(d):
        chip = lax.rem(me + d, chips)
        return (t, (chip // n_w) * 2 + core, lax.rem(chip, n_w))

    other = (t, h + 1 - 2 * core, w)

    def target(d, on):
        chip = lax.rem(me + d, chips)
        return (chip // n_w) * 2 * n_w + on * n_w + lax.rem(chip, n_w)

    def swap(n, d):
        return pltpu.make_async_remote_copy(
            src_ref=terms.at[n, target(d, 1 - core)],
            dst_ref=pair.at[n, lax.rem(me + d, chips)],
            send_sem=pair_sems.at[0, n, d],
            recv_sem=pair_sems.at[1, n, d],
            device_id=other,
            device_id_type=MESH,
        )

    def send(n, d):
        return pltpu.make_async_remote_copy(
            src_ref=both.at[n, d],
            dst_ref=got.at[n, d],
            send_sem=ss.at[n, d],
            recv_sem=rs.at[n, d],
            device_id=place(d),
            device_id_type=MESH,
        )

    order = list(range(1, chips)) + [0]
    outs = (grad_down, grad_conv)

    def swap_all(n):
        for k in range(peers):
            terms[n, k] = flat[n, :, width * k : width * (k + 1)].astype(b16)
        for d in order:
            swap(n, d).start()

    def send_all(n):
        for d in order:
            swap(n, d).wait_recv()
            mine = terms[n, target(d, core)].astype(f32)
            summed = mine + pair[n, lax.rem(me + d, chips)].astype(f32)
            if d > 0:
                both[n, d] = summed.astype(b16)
                send(n, d).start()
            else:
                outs[n][...] = summed

    def finish(n):
        for d in range(1, chips):
            send(n, d).wait_recv()
            outs[n][...] += got[n, d].astype(f32)

    swap_all(0)
    loads[1].wait()

    for pt in range(2):
        for ph in range(2):
            total = jnp.zeros((n_t * 72, ch), f32)
            for a in (1,) if pt else (0, 2):
                for b in (1,) if ph else (0, 2):
                    j = 0 if a == 2 else 1
                    r = 0 if b == 2 else 1
                    for c in range(3):
                        lhs = dilated[j : j + n_t, r : r + 3, c].reshape(n_t * 72, ch)
                        total += dot_nt(lhs.astype(b16), weight(kd, a, b, c))
            fine[:, pt, :, ph] = total.reshape(n_t, 3, 24, ch)

    send_all(0)

    @pl.loop(0, n_t)
    def _(s):
        for k in range(2):
            f = 2 * s + k
            pre = parts[0, f, :, 0:24]
            sigma = 1.0 / (1.0 + jnp.exp(-pre))
            back = fine[s, k].reshape(6, 24, ch) * sigma * (1.0 + pre * (1.0 - sigma))
            grad[f] = jnp.where(inside, back, 0.0).astype(b16).astype(f32)
            centre = grad[f, 1:5, 1:17]
            for c in range(3):
                moved[c, f, :, 1 + c : 17 + c] = centre

    conv_side = jnp.concatenate(
        [dot_nt(pick, moved[c].reshape(frames * 96, ch).astype(b16)) for c in range(3)], axis=0
    ).astype(b16)
    for a in range(3):
        for b in range(3):
            if b == 1:
                lhs = even[a : a + frames, 48:144]
            else:
                lhs = odd[a : a + frames, 24 * b : 24 * b + 96]
            conv = dot(conv_side, lhs.reshape(frames * 96, ch))
            for c in range(3):
                at = ((a * 3 + b) * 3 + c) * ch
                flat[1, :, at : at + ch] = conv[share * c : share * (c + 1)]

    swap_all(1)

    def clip_part(c):
        total = jnp.zeros((192, ch), f32)
        for a in range(3):
            for b in range(3):
                lhs = grad[pl.ds(2 * t + 2 - a, 2), 2 - b : 6 - b].reshape(192, ch)
                total += dot_nt(lhs.astype(b16), weight(k1, a, b, c))
        parts[c, 0:2, 0:4, 0:24] = total.reshape(2, 4, 24, ch)

    clip_part(0)
    send_all(1)
    clip_part(1)
    clip_part(2)
    result = (
        parts[0, 0:2, 0:4, 2:18] + parts[1, 0:2, 0:4, 1:17] + parts[2, 0:2, 0:4, 0:16]
    )
    grad_clip[...] = result.astype(b16)
    finish(0)
    finish(1)

    for d in range(n_t):
        if d > 0:
            along[d - 1].wait_send()
        for i, (dh, dw) in enumerate(SIDES):

            @pl.when(exists(dh, dw))
            def _():
                beside(d, i).wait_send()

    for n in range(2):
        for d in range(chips):
            swap(n, d).wait_send()
            if d > 0:
                send(n, d).wait_send()


def local(clip, conv_weight, down_weight, out_cotangent):
    ch = clip.shape[-1]
    n_t, n_h, n_w = (lax.axis_size(axis) for axis in ("ta", "ha", "wa"))
    frames = 2 * n_t
    share = ch // n_t
    peers = n_h * n_w
    chips = peers // 2
    width = 27 * ch // peers
    f32, b16 = jnp.float32, jnp.bfloat16
    vmem = pl.BlockSpec(memory_space=pltpu.VMEM)
    hbm = pl.BlockSpec(memory_space=pl.ANY)
    dma = pltpu.SemaphoreType.DMA
    grad_clip, grad_conv, grad_down = pl.pallas_call(
        functools.partial(kernel, (n_t, n_h, n_w)),
        out_shape=[
            jax.ShapeDtypeStruct(clip.shape, b16),
            jax.ShapeDtypeStruct((share, width), f32),
            jax.ShapeDtypeStruct((share, width), f32),
        ],
        in_specs=[vmem, vmem, hbm, hbm],
        out_specs=[vmem] * 3,
        scratch_shapes=[
            pltpu.VMEM((27 * ch, ch), b16),
            pltpu.VMEM((27 * ch, ch), b16),
            pltpu.VMEM((n_t, 9, 16, ch), b16),
            pltpu.VMEM((n_t, 3, 16, ch), b16),
            pltpu.VMEM((2, 16, ch), f32),
            pltpu.VMEM((n_t, 2, 5, 16, ch), b16),
            pltpu.VMEM((n_t, 2, 3, 16, ch), b16),
            pltpu.VMEM((n_t, 2, 2, 2, 16, ch), b16),
            pltpu.VMEM((frames + 2, 8, 24, ch), f32),
            pltpu.VMEM((frames + 2, 192, ch), b16),
            pltpu.VMEM((frames + 2, 144, ch), b16),
            pltpu.VMEM((3, frames, 6, 32, ch), f32),
            pltpu.VMEM((n_t, 2, 3, 2, 24, ch), f32),
            pltpu.VMEM((n_t + 1, 2, 3, 2, 24, ch), f32),
            pltpu.VMEM((frames + 2, 6, 24, ch), f32),
            pltpu.VMEM((3, frames, 4, 24, ch), f32),
            pltpu.VMEM((n_t + 1, 4, 3, 24, ch), f32),
            pltpu.VMEM((3, n_t, 2, 24, ch), f32),
            pltpu.VMEM((2, share, 27 * ch), f32),
            pltpu.VMEM((2, peers, share, width), b16),
            pltpu.VMEM((2, chips, share, width), b16),
            pltpu.VMEM((2, chips, share, width), b16),
            pltpu.VMEM((2, chips, share, width), b16),
            dma((2,)),
            dma((n_t - 1,)),
            dma((n_t - 1,)),
            dma((n_t, 8)),
            dma((n_t, 8)),
            dma((2, 2, chips)),
            dma((2, chips)),
            dma((2, chips)),
        ],
        compiler_params=pltpu.CompilerParams(
            collective_id=0, has_side_effects=True, vmem_limit_bytes=56 * 2**20
        ),
    )(clip, out_cotangent, conv_weight, down_weight)
    return (grad_clip, grad_conv.T, grad_down.T)


def solution(mesh):
    return jax.shard_map(
        local,
        mesh=mesh,
        in_specs=(P("ta", "ha", "wa", None), P(), P(), P("ta", "ha", "wa", None)),
        out_specs=(P("ta", "ha", "wa", None), P(("ha", "wa"), "ta"), P(("ha", "wa"), "ta")),
        check_vma=False,
    )
```

```python
import functools

import jax
import jax.numpy as jnp
from jax import lax
from jax.experimental import pallas as pl
from jax.experimental.pallas import tpu as pltpu
from jax.sharding import PartitionSpec as P

MESH = pl.DeviceIdType.MESH
SIDES = [(dh, dw) for dh in (-1, 0, 1) for dw in (-1, 0, 1) if (dh, dw) != (0, 0)]
NT = (((1,), (1,)), ((), ()))


def dot(lhs, rhs):
    return jnp.dot(lhs, rhs, preferred_element_type=jnp.float32)


def dot_nt(lhs, rhs):
    return lax.dot_general(lhs, rhs, NT, preferred_element_type=jnp.float32)


def kernel(
    sizes, clip, cot, k1_hbm, kd_hbm, grad_clip, grad_conv, grad_down,
    k1, kd, mid, edge, strip_f32, rows, cols, diag,
    wide, even, odd, parts, fine, act, grad, moved, dilated, own_cot,
    flat, terms, pair, both, got,
    load, zs, zr, ps, pr, pair_sems, ss, rs,
):
    n_t, n_h, n_w = sizes
    frames = 2 * n_t
    t, h, w = lax.axis_index("ta"), lax.axis_index("ha"), lax.axis_index("wa")
    f32, b16 = jnp.float32, jnp.bfloat16
    ch = clip.shape[-1]
    share = ch // n_t
    peers = n_h * n_w
    chips = peers // 2
    core = lax.rem(h, 2)
    me = (h // 2) * n_w + w

    loads = [
        pltpu.make_async_copy(k1_hbm, k1, load.at[0]),
        pltpu.make_async_copy(kd_hbm, kd, load.at[1]),
    ]
    for copy in loads:
        copy.start()

    barrier = pltpu.get_barrier_semaphore()
    for d in range(1, n_t):
        pl.semaphore_signal(
            barrier, inc=1, device_id=(lax.rem(t + d, n_t), h, w), device_id_type=MESH
        )
    for d in range(1, peers):
        peer = lax.rem(h * n_w + w + d, peers)
        pl.semaphore_signal(
            barrier, inc=1, device_id=(t, peer // n_w, lax.rem(peer, n_w)), device_id_type=MESH
        )

    def exists(dh, dw):
        return (h + dh >= 0) & (h + dh < n_h) & (w + dw >= 0) & (w + dw < n_w)

    def slot(s, dh, dw):
        if dw == 0:
            return rows.at[s, 0 if dh > 0 else 1]
        if dh == 0:
            return cols.at[s, 0 if dw > 0 else 1]
        return diag.at[s, 0 if dh > 0 else 1, 0 if dw > 0 else 1]

    def piece(s, dh, dw):
        if dw == 0:
            return mid.at[s, pl.ds(0, 5) if dh < 0 else pl.ds(4, 5)]
        if dh == 0:
            return edge.at[s]
        return edge.at[s, pl.ds(0, 2) if dh < 0 else pl.ds(1, 2)]

    for f in range(2):
        for r in range(2):
            mid[t, 2 * f + r] = clip[f, r]
            mid[t, 5 + 2 * f + r] = clip[f, 2 + r]
    mid[t, 4] = cot[0].reshape(16, ch)

    def pack(s):
        for p in range(2):
            for k in range(4):
                line = mid[s, 5 * p + k].astype(f32)
                strip_f32[p, 4 * k : 4 * k + 2] = line[0:2]
                strip_f32[p, 4 * k + 2 : 4 * k + 4] = line[14:16]
            edge[s, 2 * p] = strip_f32[p].astype(b16)
        edge[s, 1] = mid[s, 4]

    pack(t)
    pl.semaphore_wait(barrier, n_t + peers - 2)

    along = []
    for d in range(1, n_t):
        copy = pltpu.make_async_remote_copy(
            src_ref=mid.at[t],
            dst_ref=mid.at[t],
            send_sem=zs.at[d - 1],
            recv_sem=zr.at[d - 1],
            device_id=(lax.rem(t + d, n_t), h, w),
            device_id_type=MESH,
        )
        copy.start()
        along.append(copy)

    def landing(d):
        s = lax.rem(t - d + n_t, n_t)
        return pltpu.make_async_remote_copy(
            src_ref=mid.at[s],
            dst_ref=mid.at[s],
            send_sem=zs.at[d - 1],
            recv_sem=zr.at[d - 1],
            device_id=(lax.rem(t + d, n_t), h, w),
            device_id_type=MESH,
        )

    def beside(d, i):
        dh, dw = SIDES[i]
        s = lax.rem(t - d + n_t, n_t)
        return pltpu.make_async_remote_copy(
            src_ref=piece(s, dh, dw),
            dst_ref=slot(s, dh, dw),
            send_sem=ps.at[d, i],
            recv_sem=pr.at[d, i],
            device_id=(t, h + dh, w + dw),
            device_id_type=MESH,
        )

    def spread_out(d):
        for i, (dh, dw) in enumerate(SIDES):

            @pl.when(exists(dh, dw))
            def _():
                beside(d, i).start()

    def collect(d):
        for i, (dh, dw) in enumerate(SIDES):

            @pl.when(exists(-dh, -dw))
            def _():
                beside(d, i).wait_recv()

    spread_out(0)
    for i, (dh, dw) in enumerate(SIDES):

        @pl.when(jnp.logical_not(exists(-dh, -dw)))
        def _():
            for block in range(n_t):
                target = slot(block, dh, dw)
                target[...] = jnp.zeros(target.shape, target.dtype)

    wide[0:2] = jnp.zeros((2, 8, 24, ch), f32)
    grad[frames : frames + 2] = jnp.zeros((2, 6, 24, ch), f32)
    act[0:1] = jnp.zeros((1,) + act.shape[1:], f32)
    dilated[n_t : n_t + 1] = jnp.zeros((1,) + dilated.shape[1:], f32)
    moved[...] = jnp.zeros(moved.shape, f32)

    out_at = lax.broadcasted_iota(jnp.int32, (72, 24), 0)
    in_at = lax.broadcasted_iota(jnp.int32, (72, 24), 1)
    tap = jnp.where(out_at >= 48, 2, jnp.where(out_at >= 24, 1, 0))
    reach = out_at - 24 * tap - tap
    hit = (reach == 2 * (in_at - 8))
    select = jnp.where(hit, 1.0, 0.0).astype(b16)
    select_own = jnp.where(hit & (in_at >= 8) & (in_at < 16), 1.0, 0.0).astype(b16)

    def fill(s):
        for f in range(2):
            for r in range(2):
                at, k = 2 + 2 * s + f, 2 * f + r
                wide[at, r, 2:18] = rows[s, 0, 1 + k].astype(f32)
                wide[at, 2 + r, 2:18] = mid[s, k].astype(f32)
                wide[at, 4 + r, 2:18] = mid[s, 5 + k].astype(f32)
                wide[at, 6 + r, 2:18] = rows[s, 1, k].astype(f32)
        for side in range(2):
            strips = (diag[s, 0, side, 1], cols[s, side, 0], cols[s, side, 2], diag[s, 1, side, 0])
            for n, strip in enumerate(strips):
                strip = strip.astype(f32)
                for f in range(2):
                    for r in range(2):
                        first = 4 * (2 * f + r) + 2 - 2 * side
                        wide[2 + 2 * s + f, 2 * n + r, 18 * side : 18 * side + 2] = strip[
                            first : first + 2
                        ]
        middle = (
            (diag[s, 0, 0, 0], rows[s, 0, 0], diag[s, 0, 1, 0]),
            (cols[s, 0, 1], mid[s, 4], cols[s, 1, 1]),
            (diag[s, 1, 0, 1], rows[s, 1, 4], diag[s, 1, 1, 1]),
        )
        for n, (block, r) in enumerate(((0, 1), (1, 0), (1, 1), (2, 0))):
            line = jnp.concatenate(
                [x.astype(f32)[8 * r : 8 * r + 8] for x in middle[block]], axis=0
            ).astype(b16)
            spread = dot(select, line)
            for c in range(3):
                dilated[s, n, c] = spread[24 * c : 24 * c + 24]
            if block == 1:
                spread = dot(select_own, line)
                for c in range(3):
                    own_cot[c, s, r] = spread[24 * c : 24 * c + 24]

    def stack(f):
        even[f] = wide[f].reshape(192, ch).astype(b16)
        odd[f] = wide[f, 1:7].reshape(144, ch).astype(b16)

    def shifted(f, count, b):
        if b == 1:
            return odd[pl.ds(f, count)].reshape(count * 144, ch)
        return even[pl.ds(f, count), 24 * b : 24 * b + 144].reshape(count * 144, ch)

    def weight(ref, a, b, c):
        return ref[pl.ds(((a * 3 + b) * 3 + c) * ch, ch), :]

    def block_pre(s):
        for c in range(3):
            total = jnp.zeros((288, ch), f32)
            for a in range(3):
                for b in range(3):
                    total += dot(shifted(2 * s + a, 2, b), weight(k1, a, b, c))
            parts[c, pl.ds(2 * s, 2), :, 0:24] = total.reshape(2, 6, 24, ch)

    stack(0)
    stack(1)
    for d in range(1, n_t + 1):
        if d < n_t:
            landing(d).wait_recv()
            pack(lax.rem(t - d + n_t, n_t))
            spread_out(d)
        collect(d - 1)
        block = lax.rem(t - d + 1 + n_t, n_t)
        fill(block)
        stack(2 + 2 * block)
        stack(3 + 2 * block)
        if d == 1:
            loads[0].wait()
        elif d < n_t:
            block_pre(lax.rem(t - d + 2 + n_t, n_t))

    @pl.loop(0, 2)
    def _(n):
        block_pre(lax.rem(t + 1 + n, n_t))

    row = lax.broadcasted_iota(jnp.int32, (6, 24, ch), 0) + (h * 4 - 1)
    place = lax.broadcasted_iota(jnp.int32, (6, 24, ch), 1)
    col = place + (w * 16 - 1)
    inside = (row >= 0) & (row < 4 * n_h) & (col >= 0) & (col < 16 * n_w) & (place < 18)

    @pl.loop(0, n_t)
    def _(s):
        for k in range(2):
            f = 2 * s + k
            pre = parts[0, f, :, 0:24] + parts[1, f, :, 1:25] + parts[2, f, :, 2:26]
            parts[0, f, :, 0:24] = pre
            sigma = 1.0 / (1.0 + jnp.exp(-pre))
            value = jnp.where(inside, pre * sigma, 0.0)
            act[s + 1, k] = value.astype(b16).astype(f32).reshape(3, 2, 24, ch)

    pick = (
        lax.broadcasted_iota(jnp.int32, (share, ch), 1)
        == lax.broadcasted_iota(jnp.int32, (share, ch), 0) + t * share
    )
    pick = jnp.where(pick, 1.0, 0.0).astype(b16)
    width = 27 * ch // peers
    down_side = jnp.concatenate(
        [dot_nt(pick, own_cot[c].reshape(n_t * 48, ch).astype(b16)) for c in range(3)], axis=0
    ).astype(b16)
    def place(d):
        chip = lax.rem(me + d, chips)
        return (t, (chip // n_w) * 2 + core, lax.rem(chip, n_w))

    other = (t, h + 1 - 2 * core, w)

    def target(chip, on):
        return (chip // n_w) * 2 * n_w + on * n_w + chip % n_w

    def swap(n, chip):
        return pltpu.make_async_remote_copy(
            src_ref=terms.at[n, target(chip, 1 - core)],
            dst_ref=pair.at[n, chip],
            send_sem=pair_sems.at[0, n, chip],
            recv_sem=pair_sems.at[1, n, chip],
            device_id=other,
            device_id_type=MESH,
        )

    def send(n, d):
        return pltpu.make_async_remote_copy(
            src_ref=both.at[n, d],
            dst_ref=got.at[n, d],
            send_sem=ss.at[n, d],
            recv_sem=rs.at[n, d],
            device_id=place(d),
            device_id_type=MESH,
        )

    order = list(range(1, chips)) + [0]
    outs = (grad_down, grad_conv)

    def swap_ready(n, before, done):
        for chip in range(chips):
            last = target(chip, 1)
            if before < width * (last + 1) <= done:
                for k in (target(chip, 0), last):
                    terms[n, k] = flat[n, :, width * k : width * (k + 1)].astype(b16)
                swap(n, chip).start()

    def send_all(n):
        for d in order:
            chip = lax.rem(me + d, chips)
            swap(n, chip).wait_recv()
            mine = terms[n, target(chip, core)].astype(f32)
            summed = mine + pair[n, chip].astype(f32)
            if d > 0:
                both[n, d] = summed.astype(b16)
                send(n, d).start()
            else:
                outs[n][...] = summed

    def finish(n):
        for d in range(1, chips):
            send(n, d).wait_recv()
            outs[n][...] += got[n, d].astype(f32)

    for a in range(3):
        for b in range(3):
            lhs = act[a // 2 : a // 2 + n_t, a % 2, b // 2 : b // 2 + 2, b % 2]
            down = dot(down_side, lhs.reshape(n_t * 48, ch).astype(b16))
            for c in range(3):
                at = ((a * 3 + b) * 3 + c) * ch
                flat[0, :, at : at + ch] = down[share * c : share * (c + 1)]
            swap_ready(0, (a * 3 + b) * 3 * ch, (a * 3 + b + 1) * 3 * ch)

    loads[1].wait()

    for pt in range(2):
        for ph in range(2):
            total = jnp.zeros((n_t * 72, ch), f32)
            for a in (1,) if pt else (0, 2):
                for b in (1,) if ph else (0, 2):
                    j = 0 if a == 2 else 1
                    r = 0 if b == 2 else 1
                    for c in range(3):
                        lhs = dilated[j : j + n_t, r : r + 3, c].reshape(n_t * 72, ch)
                        total += dot_nt(lhs.astype(b16), weight(kd, a, b, c))
            fine[:, pt, :, ph] = total.reshape(n_t, 3, 24, ch)

    send_all(0)

    @pl.loop(0, n_t)
    def _(s):
        for k in range(2):
            f = 2 * s + k
            pre = parts[0, f, :, 0:24]
            sigma = 1.0 / (1.0 + jnp.exp(-pre))
            back = fine[s, k].reshape(6, 24, ch) * sigma * (1.0 + pre * (1.0 - sigma))
            grad[f] = jnp.where(inside, back, 0.0).astype(b16).astype(f32)
            centre = grad[f, 1:5, 1:17]
            for c in range(3):
                moved[c, f, :, 1 + c : 17 + c] = centre

    conv_side = jnp.concatenate(
        [dot_nt(pick, moved[c].reshape(frames * 96, ch).astype(b16)) for c in range(3)], axis=0
    ).astype(b16)
    for a in range(3):
        for b in range(3):
            if b == 1:
                lhs = even[a : a + frames, 48:144]
            else:
                lhs = odd[a : a + frames, 24 * b : 24 * b + 96]
            conv = dot(conv_side, lhs.reshape(frames * 96, ch))
            for c in range(3):
                at = ((a * 3 + b) * 3 + c) * ch
                flat[1, :, at : at + ch] = conv[share * c : share * (c + 1)]
            swap_ready(1, (a * 3 + b) * 3 * ch, (a * 3 + b + 1) * 3 * ch)

    def clip_part(c):
        total = jnp.zeros((192, ch), f32)
        for a in range(3):
            for b in range(3):
                lhs = grad[pl.ds(2 * t + 2 - a, 2), 2 - b : 6 - b].reshape(192, ch)
                total += dot_nt(lhs.astype(b16), weight(k1, a, b, c))
        parts[c, 0:2, 0:4, 0:24] = total.reshape(2, 4, 24, ch)

    clip_part(0)
    send_all(1)
    clip_part(1)
    clip_part(2)
    result = (
        parts[0, 0:2, 0:4, 2:18] + parts[1, 0:2, 0:4, 1:17] + parts[2, 0:2, 0:4, 0:16]
    )
    grad_clip[...] = result.astype(b16)
    finish(0)
    finish(1)

    for d in range(n_t):
        if d > 0:
            along[d - 1].wait_send()
        for i, (dh, dw) in enumerate(SIDES):

            @pl.when(exists(dh, dw))
            def _():
                beside(d, i).wait_send()

    for n in range(2):
        for d in range(chips):
            swap(n, d).wait_send()
            if d > 0:
                send(n, d).wait_send()


def hand_over(a_in, b_in, c_in, a_out, b_out, c_out, sems):
    copies = [
        pltpu.make_async_copy(source, place, sems.at[n])
        for n, (source, place) in enumerate(((a_in, a_out), (b_in, b_out), (c_in, c_out)))
    ]
    for copy in copies:
        copy.start()
    for copy in copies:
        copy.wait()


def local(clip, conv_weight, down_weight, out_cotangent):
    ch = clip.shape[-1]
    n_t, n_h, n_w = (lax.axis_size(axis) for axis in ("ta", "ha", "wa"))
    frames = 2 * n_t
    share = ch // n_t
    peers = n_h * n_w
    chips = peers // 2
    width = 27 * ch // peers
    f32, b16 = jnp.float32, jnp.bfloat16
    vmem = pl.BlockSpec(memory_space=pltpu.VMEM)
    hbm = pl.BlockSpec(memory_space=pl.ANY)
    dma = pltpu.SemaphoreType.DMA
    grad_clip, grad_conv, grad_down = pl.pallas_call(
        functools.partial(kernel, (n_t, n_h, n_w)),
        out_shape=[
            jax.ShapeDtypeStruct(clip.shape, b16),
            jax.ShapeDtypeStruct((share, width), f32),
            jax.ShapeDtypeStruct((share, width), f32),
        ],
        in_specs=[vmem, vmem, hbm, hbm],
        out_specs=[vmem] * 3,
        scratch_shapes=[
            pltpu.VMEM((27 * ch, ch), b16),
            pltpu.VMEM((27 * ch, ch), b16),
            pltpu.VMEM((n_t, 9, 16, ch), b16),
            pltpu.VMEM((n_t, 3, 16, ch), b16),
            pltpu.VMEM((2, 16, ch), f32),
            pltpu.VMEM((n_t, 2, 5, 16, ch), b16),
            pltpu.VMEM((n_t, 2, 3, 16, ch), b16),
            pltpu.VMEM((n_t, 2, 2, 2, 16, ch), b16),
            pltpu.VMEM((frames + 2, 8, 24, ch), f32),
            pltpu.VMEM((frames + 2, 192, ch), b16),
            pltpu.VMEM((frames + 2, 144, ch), b16),
            pltpu.VMEM((3, frames, 6, 32, ch), f32),
            pltpu.VMEM((n_t, 2, 3, 2, 24, ch), f32),
            pltpu.VMEM((n_t + 1, 2, 3, 2, 24, ch), f32),
            pltpu.VMEM((frames + 2, 6, 24, ch), f32),
            pltpu.VMEM((3, frames, 4, 24, ch), f32),
            pltpu.VMEM((n_t + 1, 4, 3, 24, ch), f32),
            pltpu.VMEM((3, n_t, 2, 24, ch), f32),
            pltpu.VMEM((2, share, 27 * ch), f32),
            pltpu.VMEM((2, peers, share, width), b16),
            pltpu.VMEM((2, chips, share, width), b16),
            pltpu.VMEM((2, chips, share, width), b16),
            pltpu.VMEM((2, chips, share, width), b16),
            dma((2,)),
            dma((n_t - 1,)),
            dma((n_t - 1,)),
            dma((n_t, 8)),
            dma((n_t, 8)),
            dma((2, 2, chips)),
            dma((2, chips)),
            dma((2, chips)),
        ],
        compiler_params=pltpu.CompilerParams(
            collective_id=0, has_side_effects=True, vmem_limit_bytes=53 * 2**20
        ),
    )(clip, out_cotangent, conv_weight, down_weight)
    grad_clip, grad_conv, grad_down = pl.pallas_call(
        hand_over,
        out_shape=[jax.ShapeDtypeStruct(x.shape, x.dtype) for x in (grad_clip, grad_conv, grad_down)],
        in_specs=[hbm] * 3,
        out_specs=[hbm] * 3,
        scratch_shapes=[dma((3,))],
    )(grad_clip, grad_conv, grad_down)
    return (grad_clip, grad_conv.T, grad_down.T)


def solution(mesh):
    return jax.shard_map(
        local,
        mesh=mesh,
        in_specs=(P("ta", "ha", "wa", None), P(), P(), P("ta", "ha", "wa", None)),
        out_specs=(P("ta", "ha", "wa", None), P(("ha", "wa"), "ta"), P(("ha", "wa"), "ta")),
        check_vma=False,
    )
```

```python
import functools

import jax
import jax.numpy as jnp
from jax import lax
from jax.experimental import pallas as pl
from jax.experimental.pallas import tpu as pltpu
from jax.sharding import PartitionSpec as P

MESH = pl.DeviceIdType.MESH
SIDES = [(dh, dw) for dh in (-1, 0, 1) for dw in (-1, 0, 1) if (dh, dw) != (0, 0)]
NT = (((1,), (1,)), ((), ()))


def dot(lhs, rhs):
    return jnp.dot(lhs, rhs, preferred_element_type=jnp.float32)


def dot_nt(lhs, rhs):
    return lax.dot_general(lhs, rhs, NT, preferred_element_type=jnp.float32)


def kernel(
    sizes, clip, cot, k1_hbm, kd_hbm, grad_clip, grad_conv, grad_down,
    k1, kd, mid, edge, strip_f32, rows, cols, diag,
    wide, even, odd, parts, fine, act, grad, moved, dilated, own_cot,
    flat, terms, pair, both, got,
    load, zs, zr, ps, pr, pair_sems, ss, rs,
):
    n_t, n_h, n_w = sizes
    frames = 2 * n_t
    t, h, w = lax.axis_index("ta"), lax.axis_index("ha"), lax.axis_index("wa")
    f32, b16 = jnp.float32, jnp.bfloat16
    ch = clip.shape[-1]
    share = ch // n_t
    peers = n_h * n_w
    chips = peers // 2
    core = lax.rem(h, 2)
    me = (h // 2) * n_w + w

    loads = [
        pltpu.make_async_copy(k1_hbm, k1, load.at[0]),
        pltpu.make_async_copy(kd_hbm, kd, load.at[1]),
    ]
    for copy in loads:
        copy.start()

    barrier = pltpu.get_barrier_semaphore()
    for d in range(1, n_t):
        pl.semaphore_signal(
            barrier, inc=1, device_id=(lax.rem(t + d, n_t), h, w), device_id_type=MESH
        )
    for d in range(1, peers):
        peer = lax.rem(h * n_w + w + d, peers)
        pl.semaphore_signal(
            barrier, inc=1, device_id=(t, peer // n_w, lax.rem(peer, n_w)), device_id_type=MESH
        )

    def exists(dh, dw):
        return (h + dh >= 0) & (h + dh < n_h) & (w + dw >= 0) & (w + dw < n_w)

    def slot(s, dh, dw):
        if dw == 0:
            return rows.at[s, 0 if dh > 0 else 1]
        if dh == 0:
            return cols.at[s, 0 if dw > 0 else 1]
        return diag.at[s, 0 if dh > 0 else 1, 0 if dw > 0 else 1]

    def piece(s, dh, dw):
        if dw == 0:
            return mid.at[s, pl.ds(0, 5) if dh < 0 else pl.ds(4, 5)]
        if dh == 0:
            return edge.at[s]
        return edge.at[s, pl.ds(0, 2) if dh < 0 else pl.ds(1, 2)]

    for f in range(2):
        for r in range(2):
            mid[t, 2 * f + r] = clip[f, r]
            mid[t, 5 + 2 * f + r] = clip[f, 2 + r]
    mid[t, 4] = cot[0].reshape(16, ch)

    def pack(s):
        for p in range(2):
            for k in range(4):
                line = mid[s, 5 * p + k].astype(f32)
                strip_f32[p, 4 * k : 4 * k + 2] = line[0:2]
                strip_f32[p, 4 * k + 2 : 4 * k + 4] = line[14:16]
            edge[s, 2 * p] = strip_f32[p].astype(b16)
        edge[s, 1] = mid[s, 4]

    pack(t)
    pl.semaphore_wait(barrier, n_t + peers - 2)

    along = []
    for d in range(1, n_t):
        copy = pltpu.make_async_remote_copy(
            src_ref=mid.at[t],
            dst_ref=mid.at[t],
            send_sem=zs.at[d - 1],
            recv_sem=zr.at[d - 1],
            device_id=(lax.rem(t + d, n_t), h, w),
            device_id_type=MESH,
        )
        copy.start()
        along.append(copy)

    def landing(d):
        s = lax.rem(t - d + n_t, n_t)
        return pltpu.make_async_remote_copy(
            src_ref=mid.at[s],
            dst_ref=mid.at[s],
            send_sem=zs.at[d - 1],
            recv_sem=zr.at[d - 1],
            device_id=(lax.rem(t + d, n_t), h, w),
            device_id_type=MESH,
        )

    def beside(d, i):
        dh, dw = SIDES[i]
        s = lax.rem(t - d + n_t, n_t)
        return pltpu.make_async_remote_copy(
            src_ref=piece(s, dh, dw),
            dst_ref=slot(s, dh, dw),
            send_sem=ps.at[d, i],
            recv_sem=pr.at[d, i],
            device_id=(t, h + dh, w + dw),
            device_id_type=MESH,
        )

    def spread_out(d):
        for i, (dh, dw) in enumerate(SIDES):

            @pl.when(exists(dh, dw))
            def _():
                beside(d, i).start()

    def collect(d):
        for i, (dh, dw) in enumerate(SIDES):

            @pl.when(exists(-dh, -dw))
            def _():
                beside(d, i).wait_recv()

    spread_out(0)
    for i, (dh, dw) in enumerate(SIDES):

        @pl.when(jnp.logical_not(exists(-dh, -dw)))
        def _():
            for block in range(n_t):
                target = slot(block, dh, dw)
                target[...] = jnp.zeros(target.shape, target.dtype)

    wide[0:2] = jnp.zeros((2, 8, 24, ch), f32)
    grad[frames : frames + 2] = jnp.zeros((2, 6, 24, ch), f32)
    act[0:1] = jnp.zeros((1,) + act.shape[1:], f32)
    dilated[n_t : n_t + 1] = jnp.zeros((1,) + dilated.shape[1:], f32)
    moved[...] = jnp.zeros(moved.shape, f32)

    out_at = lax.broadcasted_iota(jnp.int32, (72, 24), 0)
    in_at = lax.broadcasted_iota(jnp.int32, (72, 24), 1)
    tap = jnp.where(out_at >= 48, 2, jnp.where(out_at >= 24, 1, 0))
    reach = out_at - 24 * tap - tap
    hit = (reach == 2 * (in_at - 8))
    select = jnp.where(hit, 1.0, 0.0).astype(b16)
    select_own = jnp.where(hit & (in_at >= 8) & (in_at < 16), 1.0, 0.0).astype(b16)

    def fill(s):
        for f in range(2):
            for r in range(2):
                at, k = 2 + 2 * s + f, 2 * f + r
                wide[at, r, 2:18] = rows[s, 0, 1 + k].astype(f32)
                wide[at, 2 + r, 2:18] = mid[s, k].astype(f32)
                wide[at, 4 + r, 2:18] = mid[s, 5 + k].astype(f32)
                wide[at, 6 + r, 2:18] = rows[s, 1, k].astype(f32)
        for side in range(2):
            strips = (diag[s, 0, side, 1], cols[s, side, 0], cols[s, side, 2], diag[s, 1, side, 0])
            for n, strip in enumerate(strips):
                strip = strip.astype(f32)
                for f in range(2):
                    for r in range(2):
                        first = 4 * (2 * f + r) + 2 - 2 * side
                        wide[2 + 2 * s + f, 2 * n + r, 18 * side : 18 * side + 2] = strip[
                            first : first + 2
                        ]
        middle = (
            (diag[s, 0, 0, 0], rows[s, 0, 0], diag[s, 0, 1, 0]),
            (cols[s, 0, 1], mid[s, 4], cols[s, 1, 1]),
            (diag[s, 1, 0, 1], rows[s, 1, 4], diag[s, 1, 1, 1]),
        )
        for n, (block, r) in enumerate(((0, 1), (1, 0), (1, 1), (2, 0))):
            line = jnp.concatenate(
                [x.astype(f32)[8 * r : 8 * r + 8] for x in middle[block]], axis=0
            ).astype(b16)
            spread = dot(select, line)
            for c in range(3):
                dilated[s, n, c] = spread[24 * c : 24 * c + 24]
            if block == 1:
                spread = dot(select_own, line)
                for c in range(3):
                    own_cot[c, s, r] = spread[24 * c : 24 * c + 24]

    def stack(f):
        even[f] = wide[f].reshape(192, ch).astype(b16)
        odd[f] = wide[f, 1:7].reshape(144, ch).astype(b16)

    def shifted(f, count, b):
        if b == 1:
            return odd[pl.ds(f, count)].reshape(count * 144, ch)
        return even[pl.ds(f, count), 24 * b : 24 * b + 144].reshape(count * 144, ch)

    def weight(ref, a, b, c):
        return ref[pl.ds(((a * 3 + b) * 3 + c) * ch, ch), :]

    def block_pre(s):
        for c in range(3):
            total = jnp.zeros((288, ch), f32)
            for a in range(3):
                for b in range(3):
                    total += dot(shifted(2 * s + a, 2, b), weight(k1, a, b, c))
            parts[c, pl.ds(2 * s, 2), :, 0:24] = total.reshape(2, 6, 24, ch)

    stack(0)
    stack(1)
    for d in range(1, n_t + 1):
        if d < n_t:
            landing(d).wait_recv()
            pack(lax.rem(t - d + n_t, n_t))
            spread_out(d)
        collect(d - 1)
        block = lax.rem(t - d + 1 + n_t, n_t)
        fill(block)
        stack(2 + 2 * block)
        stack(3 + 2 * block)
        if d == 1:
            loads[0].wait()
        elif d < n_t:
            block_pre(lax.rem(t - d + 2 + n_t, n_t))

    @pl.loop(0, 2)
    def _(n):
        block_pre(lax.rem(t + 1 + n, n_t))

    row = lax.broadcasted_iota(jnp.int32, (6, 24, ch), 0) + (h * 4 - 1)
    place = lax.broadcasted_iota(jnp.int32, (6, 24, ch), 1)
    col = place + (w * 16 - 1)
    inside = (row >= 0) & (row < 4 * n_h) & (col >= 0) & (col < 16 * n_w) & (place < 18)

    @pl.loop(0, n_t)
    def _(s):
        for k in range(2):
            f = 2 * s + k
            pre = parts[0, f, :, 0:24] + parts[1, f, :, 1:25] + parts[2, f, :, 2:26]
            parts[0, f, :, 0:24] = pre
            sigma = 1.0 / (1.0 + jnp.exp(-pre))
            value = jnp.where(inside, pre * sigma, 0.0)
            act[s + 1, k] = value.astype(b16).astype(f32).reshape(3, 2, 24, ch)

    pick = (
        lax.broadcasted_iota(jnp.int32, (share, ch), 1)
        == lax.broadcasted_iota(jnp.int32, (share, ch), 0) + t * share
    )
    pick = jnp.where(pick, 1.0, 0.0).astype(b16)
    width = 27 * ch // peers
    down_side = jnp.concatenate(
        [dot_nt(pick, own_cot[c].reshape(n_t * 48, ch).astype(b16)) for c in range(3)], axis=0
    ).astype(b16)
    def place(d):
        chip = lax.rem(me + d, chips)
        return (t, (chip // n_w) * 2 + core, lax.rem(chip, n_w))

    other = (t, h + 1 - 2 * core, w)

    def target(chip, on):
        return (chip // n_w) * 2 * n_w + on * n_w + chip % n_w

    def swap(n, chip):
        return pltpu.make_async_remote_copy(
            src_ref=terms.at[n, target(chip, 1 - core)],
            dst_ref=pair.at[n, chip],
            send_sem=pair_sems.at[0, n, chip],
            recv_sem=pair_sems.at[1, n, chip],
            device_id=other,
            device_id_type=MESH,
        )

    def send(n, d):
        return pltpu.make_async_remote_copy(
            src_ref=both.at[n, d],
            dst_ref=got.at[n, d],
            send_sem=ss.at[n, d],
            recv_sem=rs.at[n, d],
            device_id=place(d),
            device_id_type=MESH,
        )

    order = list(range(1, chips)) + [0]
    outs = (grad_down, grad_conv)

    def swap_ready(n, before, done):
        for chip in range(chips):
            last = target(chip, 1)
            if before < width * (last + 1) <= done:
                for k in (target(chip, 0), last):
                    terms[n, k] = flat[n, :, width * k : width * (k + 1)].astype(b16)
                swap(n, chip).start()

    def send_all(n):
        for d in order:
            chip = lax.rem(me + d, chips)
            swap(n, chip).wait_recv()
            mine = terms[n, target(chip, core)].astype(f32)
            summed = mine + pair[n, chip].astype(f32)
            if d > 0:
                both[n, d] = summed.astype(b16)
                send(n, d).start()
            else:
                outs[n][...] = summed

    def finish(n):
        for d in range(1, chips):
            send(n, d).wait_recv()
            outs[n][...] += got[n, d].astype(f32)

    for a in range(3):
        for b in range(3):
            lhs = act[a // 2 : a // 2 + n_t, a % 2, b // 2 : b // 2 + 2, b % 2]
            down = dot(down_side, lhs.reshape(n_t * 48, ch).astype(b16))
            for c in range(3):
                at = ((a * 3 + b) * 3 + c) * ch
                flat[0, :, at : at + ch] = down[share * c : share * (c + 1)]
            swap_ready(0, (a * 3 + b) * 3 * ch, (a * 3 + b + 1) * 3 * ch)

    loads[1].wait()

    for pt in range(2):
        for ph in range(2):
            total = jnp.zeros((n_t * 72, ch), f32)
            for a in (1,) if pt else (0, 2):
                for b in (1,) if ph else (0, 2):
                    j = 0 if a == 2 else 1
                    r = 0 if b == 2 else 1
                    for c in range(3):
                        lhs = dilated[j : j + n_t, r : r + 3, c].reshape(n_t * 72, ch)
                        total += dot_nt(lhs.astype(b16), weight(kd, a, b, c))
            fine[:, pt, :, ph] = total.reshape(n_t, 3, 24, ch)
        if pt == 0:
            send_all(0)

    @pl.loop(0, n_t)
    def _(s):
        for k in range(2):
            f = 2 * s + k
            pre = parts[0, f, :, 0:24]
            sigma = 1.0 / (1.0 + jnp.exp(-pre))
            back = fine[s, k].reshape(6, 24, ch) * sigma * (1.0 + pre * (1.0 - sigma))
            grad[f] = jnp.where(inside, back, 0.0).astype(b16).astype(f32)
            centre = grad[f, 1:5, 1:17]
            for c in range(3):
                moved[c, f, :, 1 + c : 17 + c] = centre

    conv_side = jnp.concatenate(
        [dot_nt(pick, moved[c].reshape(frames * 96, ch).astype(b16)) for c in range(3)], axis=0
    ).astype(b16)
    for a in range(3):
        for b in range(3):
            if b == 1:
                lhs = even[a : a + frames, 48:144]
            else:
                lhs = odd[a : a + frames, 24 * b : 24 * b + 96]
            conv = dot(conv_side, lhs.reshape(frames * 96, ch))
            for c in range(3):
                at = ((a * 3 + b) * 3 + c) * ch
                flat[1, :, at : at + ch] = conv[share * c : share * (c + 1)]
            swap_ready(1, (a * 3 + b) * 3 * ch, (a * 3 + b + 1) * 3 * ch)

    def clip_part(c):
        total = jnp.zeros((192, ch), f32)
        for a in range(3):
            for b in range(3):
                lhs = grad[pl.ds(2 * t + 2 - a, 2), 2 - b : 6 - b].reshape(192, ch)
                total += dot_nt(lhs.astype(b16), weight(k1, a, b, c))
        parts[c, 0:2, 0:4, 0:24] = total.reshape(2, 4, 24, ch)

    clip_part(0)
    send_all(1)
    clip_part(1)
    clip_part(2)
    result = (
        parts[0, 0:2, 0:4, 2:18] + parts[1, 0:2, 0:4, 1:17] + parts[2, 0:2, 0:4, 0:16]
    )
    grad_clip[...] = result.astype(b16)
    finish(0)
    finish(1)

    for d in range(n_t):
        if d > 0:
            along[d - 1].wait_send()
        for i, (dh, dw) in enumerate(SIDES):

            @pl.when(exists(dh, dw))
            def _():
                beside(d, i).wait_send()

    for n in range(2):
        for d in range(chips):
            swap(n, d).wait_send()
            if d > 0:
                send(n, d).wait_send()


def hand_over(a_in, b_in, c_in, a_out, b_out, c_out):
    a_out[...] = a_in[...]
    b_out[...] = b_in[...]
    c_out[...] = c_in[...]


def local(clip, conv_weight, down_weight, out_cotangent):
    ch = clip.shape[-1]
    n_t, n_h, n_w = (lax.axis_size(axis) for axis in ("ta", "ha", "wa"))
    frames = 2 * n_t
    share = ch // n_t
    peers = n_h * n_w
    chips = peers // 2
    width = 27 * ch // peers
    f32, b16 = jnp.float32, jnp.bfloat16
    vmem = pl.BlockSpec(memory_space=pltpu.VMEM)
    hbm = pl.BlockSpec(memory_space=pl.ANY)
    dma = pltpu.SemaphoreType.DMA
    grad_clip, grad_conv, grad_down = pl.pallas_call(
        functools.partial(kernel, (n_t, n_h, n_w)),
        out_shape=[
            jax.ShapeDtypeStruct(clip.shape, b16),
            jax.ShapeDtypeStruct((share, width), f32),
            jax.ShapeDtypeStruct((share, width), f32),
        ],
        in_specs=[vmem, vmem, hbm, hbm],
        out_specs=[vmem] * 3,
        scratch_shapes=[
            pltpu.VMEM((27 * ch, ch), b16),
            pltpu.VMEM((27 * ch, ch), b16),
            pltpu.VMEM((n_t, 9, 16, ch), b16),
            pltpu.VMEM((n_t, 3, 16, ch), b16),
            pltpu.VMEM((2, 16, ch), f32),
            pltpu.VMEM((n_t, 2, 5, 16, ch), b16),
            pltpu.VMEM((n_t, 2, 3, 16, ch), b16),
            pltpu.VMEM((n_t, 2, 2, 2, 16, ch), b16),
            pltpu.VMEM((frames + 2, 8, 24, ch), f32),
            pltpu.VMEM((frames + 2, 192, ch), b16),
            pltpu.VMEM((frames + 2, 144, ch), b16),
            pltpu.VMEM((3, frames, 6, 32, ch), f32),
            pltpu.VMEM((n_t, 2, 3, 2, 24, ch), f32),
            pltpu.VMEM((n_t + 1, 2, 3, 2, 24, ch), f32),
            pltpu.VMEM((frames + 2, 6, 24, ch), f32),
            pltpu.VMEM((3, frames, 4, 24, ch), f32),
            pltpu.VMEM((n_t + 1, 4, 3, 24, ch), f32),
            pltpu.VMEM((3, n_t, 2, 24, ch), f32),
            pltpu.VMEM((2, share, 27 * ch), f32),
            pltpu.VMEM((2, peers, share, width), b16),
            pltpu.VMEM((2, chips, share, width), b16),
            pltpu.VMEM((2, chips, share, width), b16),
            pltpu.VMEM((2, chips, share, width), b16),
            dma((2,)),
            dma((n_t - 1,)),
            dma((n_t - 1,)),
            dma((n_t, 8)),
            dma((n_t, 8)),
            dma((2, 2, chips)),
            dma((2, chips)),
            dma((2, chips)),
        ],
        compiler_params=pltpu.CompilerParams(
            collective_id=0, has_side_effects=True, vmem_limit_bytes=53 * 2**20
        ),
    )(clip, out_cotangent, conv_weight, down_weight)
    grad_clip, grad_conv, grad_down = pl.pallas_call(
        hand_over,
        out_shape=[jax.ShapeDtypeStruct(x.shape, x.dtype) for x in (grad_clip, grad_conv, grad_down)],
        in_specs=[vmem] * 3,
        out_specs=[vmem] * 3,
        compiler_params=pltpu.CompilerParams(vmem_limit_bytes=4 * 2**20),
    )(grad_clip, grad_conv, grad_down)
    return (grad_clip, grad_conv.T, grad_down.T)


def solution(mesh):
    return jax.shard_map(
        local,
        mesh=mesh,
        in_specs=(P("ta", "ha", "wa", None), P(), P(), P("ta", "ha", "wa", None)),
        out_specs=(P("ta", "ha", "wa", None), P(("ha", "wa"), "ta"), P(("ha", "wa"), "ta")),
        check_vma=False,
    )
```

```python
import functools

import jax
import jax.numpy as jnp
from jax import lax
from jax.experimental import pallas as pl
from jax.experimental.pallas import tpu as pltpu
from jax.sharding import PartitionSpec as P

MESH = pl.DeviceIdType.MESH
SIDES = [(dh, dw) for dh in (-1, 0, 1) for dw in (-1, 0, 1) if (dh, dw) != (0, 0)]
NT = (((1,), (1,)), ((), ()))


def dot(lhs, rhs):
    return jnp.dot(lhs, rhs, preferred_element_type=jnp.float32)


def dot_nt(lhs, rhs):
    return lax.dot_general(lhs, rhs, NT, preferred_element_type=jnp.float32)


def kernel(
    sizes, clip, cot, k1_hbm, kd_hbm, grad_clip, grad_conv, grad_down,
    k1, kd, mid, edge, strip_f32, rows, cols, diag,
    wide, even, odd, parts, fine, act, grad, moved, dilated, own_cot,
    flat, terms, pair, both, got,
    load, zs, zr, ps, pr, pair_sems, ss, rs,
):
    n_t, n_h, n_w = sizes
    frames = 2 * n_t
    t, h, w = lax.axis_index("ta"), lax.axis_index("ha"), lax.axis_index("wa")
    f32, b16 = jnp.float32, jnp.bfloat16
    ch = clip.shape[-1]
    share = ch // n_t
    peers = n_h * n_w
    chips = peers // 2
    core = lax.rem(h, 2)
    me = (h // 2) * n_w + w

    loads = [
        pltpu.make_async_copy(k1_hbm, k1, load.at[0]),
        pltpu.make_async_copy(kd_hbm, kd, load.at[1]),
    ]
    for copy in loads:
        copy.start()

    barrier = pltpu.get_barrier_semaphore()
    for d in range(1, n_t):
        pl.semaphore_signal(
            barrier, inc=1, device_id=(lax.rem(t + d, n_t), h, w), device_id_type=MESH
        )
    for d in range(1, peers):
        peer = lax.rem(h * n_w + w + d, peers)
        pl.semaphore_signal(
            barrier, inc=1, device_id=(t, peer // n_w, lax.rem(peer, n_w)), device_id_type=MESH
        )

    def exists(dh, dw):
        return (h + dh >= 0) & (h + dh < n_h) & (w + dw >= 0) & (w + dw < n_w)

    def slot(s, dh, dw):
        if dw == 0:
            return rows.at[s, 0 if dh > 0 else 1]
        if dh == 0:
            return cols.at[s, 0 if dw > 0 else 1]
        return diag.at[s, 0 if dh > 0 else 1, 0 if dw > 0 else 1]

    def piece(s, dh, dw):
        if dw == 0:
            return mid.at[s, pl.ds(0, 5) if dh < 0 else pl.ds(4, 5)]
        if dh == 0:
            return edge.at[s]
        return edge.at[s, pl.ds(0, 2) if dh < 0 else pl.ds(1, 2)]

    for f in range(2):
        for r in range(2):
            mid[t, 2 * f + r] = clip[f, r]
            mid[t, 5 + 2 * f + r] = clip[f, 2 + r]
    mid[t, 4] = cot[0].reshape(16, ch)

    def pack(s):
        for p in range(2):
            for k in range(4):
                line = mid[s, 5 * p + k].astype(f32)
                strip_f32[p, 4 * k : 4 * k + 2] = line[0:2]
                strip_f32[p, 4 * k + 2 : 4 * k + 4] = line[14:16]
            edge[s, 2 * p] = strip_f32[p].astype(b16)
        edge[s, 1] = mid[s, 4]

    pack(t)
    pl.semaphore_wait(barrier, n_t + peers - 2)

    along = []
    for d in range(1, n_t):
        copy = pltpu.make_async_remote_copy(
            src_ref=mid.at[t],
            dst_ref=mid.at[t],
            send_sem=zs.at[d - 1],
            recv_sem=zr.at[d - 1],
            device_id=(lax.rem(t + d, n_t), h, w),
            device_id_type=MESH,
        )
        copy.start()
        along.append(copy)

    def landing(d):
        s = lax.rem(t - d + n_t, n_t)
        return pltpu.make_async_remote_copy(
            src_ref=mid.at[s],
            dst_ref=mid.at[s],
            send_sem=zs.at[d - 1],
            recv_sem=zr.at[d - 1],
            device_id=(lax.rem(t + d, n_t), h, w),
            device_id_type=MESH,
        )

    def beside(d, i):
        dh, dw = SIDES[i]
        s = lax.rem(t - d + n_t, n_t)
        return pltpu.make_async_remote_copy(
            src_ref=piece(s, dh, dw),
            dst_ref=slot(s, dh, dw),
            send_sem=ps.at[d, i],
            recv_sem=pr.at[d, i],
            device_id=(t, h + dh, w + dw),
            device_id_type=MESH,
        )

    def spread_out(d):
        for i, (dh, dw) in enumerate(SIDES):

            @pl.when(exists(dh, dw))
            def _():
                beside(d, i).start()

    def collect(d):
        for i, (dh, dw) in enumerate(SIDES):

            @pl.when(exists(-dh, -dw))
            def _():
                beside(d, i).wait_recv()

    spread_out(0)
    for i, (dh, dw) in enumerate(SIDES):

        @pl.when(jnp.logical_not(exists(-dh, -dw)))
        def _():
            for block in range(n_t):
                target = slot(block, dh, dw)
                target[...] = jnp.zeros(target.shape, target.dtype)

    wide[0:2] = jnp.zeros((2, 8, 24, ch), f32)
    grad[frames : frames + 2] = jnp.zeros((2, 6, 24, ch), f32)
    act[0:1] = jnp.zeros((1,) + act.shape[1:], f32)
    dilated[n_t : n_t + 1] = jnp.zeros((1,) + dilated.shape[1:], f32)
    moved[...] = jnp.zeros(moved.shape, f32)

    out_at = lax.broadcasted_iota(jnp.int32, (72, 24), 0)
    in_at = lax.broadcasted_iota(jnp.int32, (72, 24), 1)
    tap = jnp.where(out_at >= 48, 2, jnp.where(out_at >= 24, 1, 0))
    reach = out_at - 24 * tap - tap
    hit = (reach == 2 * (in_at - 8))
    select = jnp.where(hit, 1.0, 0.0).astype(b16)
    select_own = jnp.where(hit & (in_at >= 8) & (in_at < 16), 1.0, 0.0).astype(b16)

    def fill(s):
        for f in range(2):
            for r in range(2):
                at, k = 2 + 2 * s + f, 2 * f + r
                wide[at, r, 2:18] = rows[s, 0, 1 + k].astype(f32)
                wide[at, 2 + r, 2:18] = mid[s, k].astype(f32)
                wide[at, 4 + r, 2:18] = mid[s, 5 + k].astype(f32)
                wide[at, 6 + r, 2:18] = rows[s, 1, k].astype(f32)
        for side in range(2):
            strips = (diag[s, 0, side, 1], cols[s, side, 0], cols[s, side, 2], diag[s, 1, side, 0])
            for n, strip in enumerate(strips):
                strip = strip.astype(f32)
                for f in range(2):
                    for r in range(2):
                        first = 4 * (2 * f + r) + 2 - 2 * side
                        wide[2 + 2 * s + f, 2 * n + r, 18 * side : 18 * side + 2] = strip[
                            first : first + 2
                        ]
        middle = (
            (diag[s, 0, 0, 0], rows[s, 0, 0], diag[s, 0, 1, 0]),
            (cols[s, 0, 1], mid[s, 4], cols[s, 1, 1]),
            (diag[s, 1, 0, 1], rows[s, 1, 4], diag[s, 1, 1, 1]),
        )
        for n, (block, r) in enumerate(((0, 1), (1, 0), (1, 1), (2, 0))):
            line = jnp.concatenate(
                [x.astype(f32)[8 * r : 8 * r + 8] for x in middle[block]], axis=0
            ).astype(b16)
            spread = dot(select, line)
            for c in range(3):
                dilated[s, n, c] = spread[24 * c : 24 * c + 24]
            if block == 1:
                spread = dot(select_own, line)
                for c in range(3):
                    own_cot[c, s, r] = spread[24 * c : 24 * c + 24]

    def stack(f):
        even[f] = wide[f].reshape(192, ch).astype(b16)
        odd[f] = wide[f, 1:7].reshape(144, ch).astype(b16)

    def shifted(f, count, b):
        if b == 1:
            return odd[pl.ds(f, count)].reshape(count * 144, ch)
        return even[pl.ds(f, count), 24 * b : 24 * b + 144].reshape(count * 144, ch)

    def weight(ref, a, b, c):
        return ref[pl.ds(((a * 3 + b) * 3 + c) * ch, ch), :]

    def block_pre(s):
        for c in range(3):
            total = jnp.zeros((288, ch), f32)
            for a in range(3):
                for b in range(3):
                    total += dot(shifted(2 * s + a, 2, b), weight(k1, a, b, c))
            parts[c, pl.ds(2 * s, 2), :, 0:24] = total.reshape(2, 6, 24, ch)

    stack(0)
    stack(1)
    for d in range(1, n_t + 1):
        if d < n_t:
            landing(d).wait_recv()
            pack(lax.rem(t - d + n_t, n_t))
            spread_out(d)
        collect(d - 1)
        block = lax.rem(t - d + 1 + n_t, n_t)
        fill(block)
        stack(2 + 2 * block)
        stack(3 + 2 * block)
        if d == 1:
            loads[0].wait()
        elif d < n_t:
            block_pre(lax.rem(t - d + 2 + n_t, n_t))

    last = [lax.rem(t + 1 + n, n_t) for n in range(2)]
    for c in range(3):
        total = jnp.zeros((576, ch), f32)
        for a in range(3):
            for b in range(3):
                lhs = jnp.concatenate([shifted(2 * s + a, 2, b) for s in last], axis=0)
                total += dot(lhs, weight(k1, a, b, c))
        for n, s in enumerate(last):
            parts[c, pl.ds(2 * s, 2), :, 0:24] = total[288 * n : 288 * n + 288].reshape(2, 6, 24, ch)

    row = lax.broadcasted_iota(jnp.int32, (6, 24, ch), 0) + (h * 4 - 1)
    place = lax.broadcasted_iota(jnp.int32, (6, 24, ch), 1)
    col = place + (w * 16 - 1)
    inside = (row >= 0) & (row < 4 * n_h) & (col >= 0) & (col < 16 * n_w) & (place < 18)

    @pl.loop(0, n_t)
    def _(s):
        for k in range(2):
            f = 2 * s + k
            pre = parts[0, f, :, 0:24] + parts[1, f, :, 1:25] + parts[2, f, :, 2:26]
            parts[0, f, :, 0:24] = pre
            sigma = 1.0 / (1.0 + jnp.exp(-pre))
            value = jnp.where(inside, pre * sigma, 0.0)
            act[s + 1, k] = value.astype(b16).astype(f32).reshape(3, 2, 24, ch)

    pick = (
        lax.broadcasted_iota(jnp.int32, (share, ch), 1)
        == lax.broadcasted_iota(jnp.int32, (share, ch), 0) + t * share
    )
    pick = jnp.where(pick, 1.0, 0.0).astype(b16)
    width = 27 * ch // peers
    down_side = jnp.concatenate(
        [dot_nt(pick, own_cot[c].reshape(n_t * 48, ch).astype(b16)) for c in range(3)], axis=0
    ).astype(b16)
    def place(d):
        chip = lax.rem(me + d, chips)
        return (t, (chip // n_w) * 2 + core, lax.rem(chip, n_w))

    other = (t, h + 1 - 2 * core, w)

    def target(chip, on):
        return (chip // n_w) * 2 * n_w + on * n_w + chip % n_w

    def swap(n, chip):
        return pltpu.make_async_remote_copy(
            src_ref=terms.at[n, target(chip, 1 - core)],
            dst_ref=pair.at[n, chip],
            send_sem=pair_sems.at[0, n, chip],
            recv_sem=pair_sems.at[1, n, chip],
            device_id=other,
            device_id_type=MESH,
        )

    def send(n, d):
        return pltpu.make_async_remote_copy(
            src_ref=both.at[n, d],
            dst_ref=got.at[n, d],
            send_sem=ss.at[n, d],
            recv_sem=rs.at[n, d],
            device_id=place(d),
            device_id_type=MESH,
        )

    order = list(range(1, chips)) + [0]
    outs = (grad_down, grad_conv)

    def swap_ready(n, before, done):
        for chip in range(chips):
            last = target(chip, 1)
            if before < width * (last + 1) <= done:
                for k in (target(chip, 0), last):
                    terms[n, k] = flat[n, :, width * k : width * (k + 1)].astype(b16)
                swap(n, chip).start()

    def send_all(n):
        for d in order:
            chip = lax.rem(me + d, chips)
            swap(n, chip).wait_recv()
            mine = terms[n, target(chip, core)].astype(f32)
            summed = mine + pair[n, chip].astype(f32)
            if d > 0:
                both[n, d] = summed.astype(b16)
                send(n, d).start()
            else:
                outs[n][...] = summed

    def finish(n):
        for d in range(1, chips):
            send(n, d).wait_recv()
            outs[n][...] += got[n, d].astype(f32)

    for a in range(3):
        for b in range(3):
            lhs = act[a // 2 : a // 2 + n_t, a % 2, b // 2 : b // 2 + 2, b % 2]
            down = dot(down_side, lhs.reshape(n_t * 48, ch).astype(b16))
            for c in range(3):
                at = ((a * 3 + b) * 3 + c) * ch
                flat[0, :, at : at + ch] = down[share * c : share * (c + 1)]
            swap_ready(0, (a * 3 + b) * 3 * ch, (a * 3 + b + 1) * 3 * ch)

    loads[1].wait()

    for pt in range(2):
        for ph in range(2):
            total = jnp.zeros((n_t * 72, ch), f32)
            for a in (1,) if pt else (0, 2):
                for b in (1,) if ph else (0, 2):
                    j = 0 if a == 2 else 1
                    r = 0 if b == 2 else 1
                    for c in range(3):
                        lhs = dilated[j : j + n_t, r : r + 3, c].reshape(n_t * 72, ch)
                        total += dot_nt(lhs.astype(b16), weight(kd, a, b, c))
            fine[:, pt, :, ph] = total.reshape(n_t, 3, 24, ch)
        if pt == 0:
            send_all(0)

    @pl.loop(0, n_t)
    def _(s):
        for k in range(2):
            f = 2 * s + k
            pre = parts[0, f, :, 0:24]
            sigma = 1.0 / (1.0 + jnp.exp(-pre))
            back = fine[s, k].reshape(6, 24, ch) * sigma * (1.0 + pre * (1.0 - sigma))
            grad[f] = jnp.where(inside, back, 0.0).astype(b16).astype(f32)
            centre = grad[f, 1:5, 1:17]
            for c in range(3):
                moved[c, f, :, 1 + c : 17 + c] = centre

    conv_side = jnp.concatenate(
        [dot_nt(pick, moved[c].reshape(frames * 96, ch).astype(b16)) for c in range(3)], axis=0
    ).astype(b16)
    for a in range(3):
        for b in range(3):
            if b == 1:
                lhs = even[a : a + frames, 48:144]
            else:
                lhs = odd[a : a + frames, 24 * b : 24 * b + 96]
            conv = dot(conv_side, lhs.reshape(frames * 96, ch))
            for c in range(3):
                at = ((a * 3 + b) * 3 + c) * ch
                flat[1, :, at : at + ch] = conv[share * c : share * (c + 1)]
            swap_ready(1, (a * 3 + b) * 3 * ch, (a * 3 + b + 1) * 3 * ch)

    def clip_part(c):
        total = jnp.zeros((192, ch), f32)
        for a in range(3):
            for b in range(3):
                lhs = grad[pl.ds(2 * t + 2 - a, 2), 2 - b : 6 - b].reshape(192, ch)
                total += dot_nt(lhs.astype(b16), weight(k1, a, b, c))
        parts[c, 0:2, 0:4, 0:24] = total.reshape(2, 4, 24, ch)

    clip_part(0)
    send_all(1)
    clip_part(1)
    finish(0)
    clip_part(2)
    result = (
        parts[0, 0:2, 0:4, 2:18] + parts[1, 0:2, 0:4, 1:17] + parts[2, 0:2, 0:4, 0:16]
    )
    grad_clip[...] = result.astype(b16)
    finish(1)

    for d in range(n_t):
        if d > 0:
            along[d - 1].wait_send()
        for i, (dh, dw) in enumerate(SIDES):

            @pl.when(exists(dh, dw))
            def _():
                beside(d, i).wait_send()

    for n in range(2):
        for d in range(chips):
            swap(n, d).wait_send()
            if d > 0:
                send(n, d).wait_send()


def hand_over(a_in, b_in, c_in, a_out, b_out, c_out):
    a_out[...] = a_in[...]
    b_out[...] = b_in[...]
    c_out[...] = c_in[...]


def local(clip, conv_weight, down_weight, out_cotangent):
    ch = clip.shape[-1]
    n_t, n_h, n_w = (lax.axis_size(axis) for axis in ("ta", "ha", "wa"))
    frames = 2 * n_t
    share = ch // n_t
    peers = n_h * n_w
    chips = peers // 2
    width = 27 * ch // peers
    f32, b16 = jnp.float32, jnp.bfloat16
    vmem = pl.BlockSpec(memory_space=pltpu.VMEM)
    hbm = pl.BlockSpec(memory_space=pl.ANY)
    dma = pltpu.SemaphoreType.DMA
    grad_clip, grad_conv, grad_down = pl.pallas_call(
        functools.partial(kernel, (n_t, n_h, n_w)),
        out_shape=[
            jax.ShapeDtypeStruct(clip.shape, b16),
            jax.ShapeDtypeStruct((share, width), f32),
            jax.ShapeDtypeStruct((share, width), f32),
        ],
        in_specs=[vmem, vmem, hbm, hbm],
        out_specs=[vmem] * 3,
        scratch_shapes=[
            pltpu.VMEM((27 * ch, ch), b16),
            pltpu.VMEM((27 * ch, ch), b16),
            pltpu.VMEM((n_t, 9, 16, ch), b16),
            pltpu.VMEM((n_t, 3, 16, ch), b16),
            pltpu.VMEM((2, 16, ch), f32),
            pltpu.VMEM((n_t, 2, 5, 16, ch), b16),
            pltpu.VMEM((n_t, 2, 3, 16, ch), b16),
            pltpu.VMEM((n_t, 2, 2, 2, 16, ch), b16),
            pltpu.VMEM((frames + 2, 8, 24, ch), f32),
            pltpu.VMEM((frames + 2, 192, ch), b16),
            pltpu.VMEM((frames + 2, 144, ch), b16),
            pltpu.VMEM((3, frames, 6, 32, ch), f32),
            pltpu.VMEM((n_t, 2, 3, 2, 24, ch), f32),
            pltpu.VMEM((n_t + 1, 2, 3, 2, 24, ch), f32),
            pltpu.VMEM((frames + 2, 6, 24, ch), f32),
            pltpu.VMEM((3, frames, 4, 24, ch), f32),
            pltpu.VMEM((n_t + 1, 4, 3, 24, ch), f32),
            pltpu.VMEM((3, n_t, 2, 24, ch), f32),
            pltpu.VMEM((2, share, 27 * ch), f32),
            pltpu.VMEM((2, peers, share, width), b16),
            pltpu.VMEM((2, chips, share, width), b16),
            pltpu.VMEM((2, chips, share, width), b16),
            pltpu.VMEM((2, chips, share, width), b16),
            dma((2,)),
            dma((n_t - 1,)),
            dma((n_t - 1,)),
            dma((n_t, 8)),
            dma((n_t, 8)),
            dma((2, 2, chips)),
            dma((2, chips)),
            dma((2, chips)),
        ],
        compiler_params=pltpu.CompilerParams(
            collective_id=0, has_side_effects=True, vmem_limit_bytes=53 * 2**20
        ),
    )(clip, out_cotangent, conv_weight, down_weight)
    grad_clip, grad_conv, grad_down = pl.pallas_call(
        hand_over,
        out_shape=[jax.ShapeDtypeStruct(x.shape, x.dtype) for x in (grad_clip, grad_conv, grad_down)],
        in_specs=[vmem] * 3,
        out_specs=[vmem] * 3,
        compiler_params=pltpu.CompilerParams(vmem_limit_bytes=4 * 2**20),
    )(grad_clip, grad_conv, grad_down)
    return (grad_clip, grad_conv.T, grad_down.T)


def solution(mesh):
    return jax.shard_map(
        local,
        mesh=mesh,
        in_specs=(P("ta", "ha", "wa", None), P(), P(), P("ta", "ha", "wa", None)),
        out_specs=(P("ta", "ha", "wa", None), P(("ha", "wa"), "ta"), P(("ha", "wa"), "ta")),
        check_vma=False,
    )
```
